128 devices in a mesh: seq: 16 (over x_hi, z, core), ch: 8 (over x_lo, y).
Axes of the slice: x: 4 (x_hi: 2, x_lo: 2; x = x_hi * 2 + x_lo), y: 4, z: 4, core: 2. Of those that a mesh axis runs over, the one named last changes fastest.
Arguments:
- proj_first: bfloat16 [16384, 1024], P('seq', 'ch'), may hold values from -6 to 6
- proj_second: bfloat16 [16384, 1024], P('seq', 'ch'), may hold values from -6 to 6
- out_gate: bfloat16 [16384, 1024], P('seq', 'ch'), may hold values from -6 to 6
- upstream: bfloat16 [16384, 1024], P('seq', 'ch'), may hold values from -6 to 6
- filter_rows: bfloat16 [16384, 1024], P('seq', 'ch'), may hold values from -2 to 2
- conv_first: float32 [3, 1024], P(None, 'ch'), may hold values from -3 to 3
- conv_second: float32 [3, 1024], P(None, 'ch'), may hold values from -3 to 3
- skip_gain: float32 [1024], P('ch'), may hold values from -4 to 4
Outputs:
- grad_first: bfloat16 [16384, 1024], P('seq', 'ch')
- grad_second: bfloat16 [16384, 1024], P('seq', 'ch')
- filter_grad: float32 [16384, 1024], P('seq', 'ch')
The draws below stay inside these ranges and needn't reach their ends.
All inputs are finite; a program needn't handle non-finite values.
Results may differ from the reference program's by a relative error of at most 0.012.
Values may be sent and summed in bfloat16 or wider, within the bound.
A program may use at most 128 MiB of HBM per device.

```python
import jax
import jax.numpy as jnp
from jax import lax

FEATURE_WIDTH = 1024
TOK_DEV = 1024
SEQUENCE_SPAN = 16384


def draw_filter_rows(key, part):
    key = jax.random.fold_in(key, 11)
    sampler_seeds = jax.random.split(key, 9)
    base = jnp.clip(jax.random.normal(sampler_seeds[0], (3, SEQUENCE_SPAN, FEATURE_WIDTH), jnp.float32), -6.0, 6.0)
    fast_share = 0.5
    fast = jax.random.uniform(sampler_seeds[1], (FEATURE_WIDTH,), jnp.float32) < fast_share
    fast_rate = 1.0 / jax.random.uniform(sampler_seeds[2], (FEATURE_WIDTH,), jnp.float32, 30.0, 50.0)
    slow_rate = jnp.exp(jax.random.uniform(sampler_seeds[3], (FEATURE_WIDTH,), jnp.float32, jnp.log(0.1), jnp.log(2.3))) / SEQUENCE_SPAN
    rate = jnp.where(fast, fast_rate, slow_rate)
    sequence_offsets = jnp.arange(SEQUENCE_SPAN, dtype=jnp.float32)[:, None]
    envelope = jnp.sqrt(1.0 - jnp.exp(-2.0 * rate)) * jnp.exp(-rate * sequence_offsets)
    regrow_gain = jnp.exp(jax.random.uniform(sampler_seeds[5], (FEATURE_WIDTH,), jnp.float32, jnp.log(0.6), jnp.log(1.2)))
    regrow_gain = jnp.where(fast, regrow_gain, 0.0) / jnp.sqrt(float(SEQUENCE_SPAN - TOK_DEV))
    regrow_env = jnp.where(sequence_offsets >= float(TOK_DEV), 1.0, 0.0) * regrow_gain
    late_reach = jnp.exp(jax.random.uniform(sampler_seeds[6], (FEATURE_WIDTH,), jnp.float32, jnp.log(30.0), jnp.log(float(max(60, SEQUENCE_SPAN // 16)))))
    late_rate = 1.0 / late_reach
    late_energy = jnp.exp(jax.random.uniform(sampler_seeds[7], (FEATURE_WIDTH,), jnp.float32, jnp.log(0.3), jnp.log(1.5)))
    late_on = jax.random.uniform(sampler_seeds[8], (FEATURE_WIDTH,), jnp.float32) < 0.5
    late_amp = jnp.where(late_on, jnp.sqrt(late_energy * (1.0 - jnp.exp(-2.0 * late_rate))), 0.0)
    late_env = late_amp * jnp.exp(-late_rate * (float(SEQUENCE_SPAN - 1) - sequence_offsets))
    contiguous_runs = jax.random.randint(sampler_seeds[4], (4, FEATURE_WIDTH), 0, SEQUENCE_SPAN)
    discarded_elements = jnp.ones((SEQUENCE_SPAN, FEATURE_WIDTH), jnp.float32)
    for lookup_slot in range(4):
        discarded_elements = discarded_elements * jnp.where(sequence_offsets >= contiguous_runs[lookup_slot].astype(jnp.float32), 0.6, 1.0)
    combined = base[0] * envelope * discarded_elements + base[1] * regrow_env + base[2] * late_env
    return jnp.clip(combined, -2.0, 2.0).astype(jnp.bfloat16)


def shard_levels(own_key, shape, pieces, least, top_value):
    def one(axis_at, shards_of):
        steps = jax.random.uniform(jax.random.fold_in(jax.random.fold_in(own_key, 6), axis_at), (shards_of,), jnp.float32, least / len(pieces), top_value / len(pieces))
        return jnp.repeat(jnp.exp(steps), shape[axis_at] // shards_of).reshape((-1,) + (1,) * (len(shape) - axis_at - 1))

    factor_of = one(*pieces[0])
    for cut in pieces[1:]:
        factor_of = factor_of * one(*cut)
    return factor_of


def scatter_about(stream_key, extent, deviation, limit, cuts=(), kind=jnp.bfloat16):
    gain = shard_levels(stream_key, extent, cuts, -0.22, 0.18) if cuts else 1.0
    drawn = jax.random.normal(stream_key, extent, jnp.float32) * deviation * gain
    return jnp.minimum(jnp.maximum(drawn, -limit), limit).astype(kind)


def setup_inputs(seed: int = 0) -> dict:
    streams_of = jax.random.split(jax.random.key(seed), 9)
    proj_first = scatter_about(streams_of[0], (SEQUENCE_SPAN, FEATURE_WIDTH), 1.0, 6.0, ((0, 16), (1, 8)))
    proj_second = scatter_about(streams_of[1], (SEQUENCE_SPAN, FEATURE_WIDTH), 1.0, 6.0, ((0, 16), (1, 8)))
    out_gate = scatter_about(streams_of[2], (SEQUENCE_SPAN, FEATURE_WIDTH), 1.0, 6.0, ((0, 16), (1, 8)))
    upstream = scatter_about(streams_of[3], (SEQUENCE_SPAN, FEATURE_WIDTH), 1.0, 6.0, ((0, 16), (1, 8)))
    filter_rows = draw_filter_rows(jax.random.fold_in(streams_of[8], 71), 0)
    conv_first = scatter_about(streams_of[5], (3, FEATURE_WIDTH), 0.6, 3.0, ((1, 8),), jnp.float32)
    conv_second = scatter_about(streams_of[6], (3, FEATURE_WIDTH), 0.6, 3.0, ((1, 8),), jnp.float32)
    skip_gain = scatter_about(streams_of[7], (FEATURE_WIDTH,), 1.0, 4.0, ((0, 8),), jnp.float32)
    return {"proj_first": proj_first, "proj_second": proj_second, "out_gate": out_gate, "upstream": upstream, "filter_rows": filter_rows, "conv_first": conv_first, "conv_second": conv_second, "skip_gain": skip_gain}


def short_forward(values, weights):
    padded = jnp.pad(values.astype(jnp.float32), ((2, 0), (0, 0)))
    return weights[0] * padded[2:] + weights[1] * padded[1:-1] + weights[2] * padded[:-2]


def short_backward(values, weights):
    padded = jnp.pad(values.astype(jnp.float32), ((0, 2), (0, 0)))
    return weights[0] * padded[:-2] + weights[1] * padded[1:-1] + weights[2] * padded[2:]


def correlate_block(blocks):
    signal, product, filter_part = blocks
    seq_len = signal.shape[-1]
    fft_len = 2 * seq_len
    spec_signal = jnp.fft.fft(signal, n=fft_len, axis=-1)
    spec_product = jnp.fft.fft(product, n=fft_len, axis=-1)
    spec_filter = jnp.fft.fft(filter_part, n=fft_len, axis=-1)
    mix_part = jnp.fft.ifft(jnp.conj(spec_filter) * spec_signal, axis=-1).real[:, :seq_len]
    corr_part = jnp.fft.ifft(jnp.conj(spec_product) * spec_signal, axis=-1).real[:, :seq_len]
    return mix_part, corr_part


def to_blocks(values):
    seq_len, chan_count = values.shape
    return values.astype(jnp.float32).T.reshape(chan_count // 128, 128, seq_len)


def from_blocks(values):
    block_count, block_size, seq_len = values.shape
    return values.reshape(block_count * block_size, seq_len).T


def reference(proj_first, proj_second, out_gate, upstream, filter_rows, conv_first, conv_second, skip_gain):
    first_conv = short_forward(proj_first, conv_first)
    second_conv = short_forward(proj_second, conv_second)
    product = (first_conv * second_conv).astype(jnp.bfloat16)
    gated_grad = (out_gate.astype(jnp.float32) * upstream.astype(jnp.float32)).astype(jnp.bfloat16)
    mix_part, corr_part = lax.map(correlate_block, (to_blocks(gated_grad), to_blocks(product), to_blocks(filter_rows)))
    mix_corr = from_blocks(mix_part).astype(jnp.bfloat16)
    filter_grad = from_blocks(corr_part) * (SEQUENCE_SPAN ** -0.5)
    mix_grad = mix_corr.astype(jnp.float32) + skip_gain * gated_grad.astype(jnp.float32)
    first_grad = (mix_grad * second_conv).astype(jnp.bfloat16)
    second_grad = (mix_grad * first_conv).astype(jnp.bfloat16)
    grad_first = short_backward(first_grad, conv_first).astype(jnp.bfloat16)
    grad_second = short_backward(second_grad, conv_second).astype(jnp.bfloat16)
    return grad_first, grad_second, filter_grad
```

```python
from functools import partial

import jax
import jax.numpy as jnp
from jax import lax
from jax.experimental import pallas as pl
from jax.experimental.pallas import tpu as pltpu
from jax.sharding import PartitionSpec as P

f32 = jnp.float32
bf16 = jnp.bfloat16
MESH = pl.DeviceIdType.MESH
N = 16
LANES = 128
TOK = 1024
EXT = TOK + 16
OWN = 8
BLOCKS = 128
EDGE = 16


def rows_of(block):
    return pl.ds(pl.multiple_of(block, 16), 16)


def kernel(
    pf, ps, og, up, fr, c1, c2, sk,
    out_first, out_second, out_filter,
    halo, sbuf, rbuf, ybuf, rmix, rcor,
    pfx, psx, fc, sc, gg, fg, sg,
    gin, fin, frp, ls, acc, y,
    halo_send, halo_recv, send_sem, recv_sem, local_sem,
):
    me = lax.axis_index("seq")
    nxt = lax.rem(me + 1, N)
    prv = lax.rem(me + N - 1, N)

    barrier = pltpu.get_barrier_semaphore()

    def greet(k, _):
        pl.semaphore_signal(
            barrier, inc=1, device_id={"seq": lax.rem(me + k, N)}, device_id_type=MESH
        )
        return 0

    lax.fori_loop(1, N, greet, 0)

    row = lax.broadcasted_iota(jnp.int32, (LANES, LANES), 0)
    col = lax.broadcasted_iota(jnp.int32, (LANES, LANES), 1)
    eye = (row == col).astype(f32).astype(bf16)
    flip = (row + col == LANES - 1).astype(f32).astype(bf16)

    def turned(block):
        return lax.dot_general(
            eye, block, (((1,), (1,)), ((), ())), preferred_element_type=f32
        )

    def flipped(block):
        back = jnp.dot(flip, block, preferred_element_type=f32).astype(bf16)
        return turned(back)

    def put(slot, pair, one, two):
        both = jnp.concatenate(
            [one.reshape(N, OWN, LANES), two.reshape(N, OWN, LANES)], axis=1
        )
        sbuf[slot, :, 16 * pair : 16 * pair + 16, :] = both.astype(bf16)

    def block(ref, i):
        return ref[LANES * i : LANES * (i + 1), :]

    def exchange(slot):
        def go(k, _):
            to = lax.rem(me + k, N)
            pltpu.make_async_remote_copy(
                src_ref=sbuf.at[slot, to],
                dst_ref=rbuf.at[slot, me],
                send_sem=send_sem.at[slot, to],
                recv_sem=recv_sem.at[slot, me],
                device_id={"seq": to},
                device_id_type=MESH,
            ).start()
            return 0

        lax.fori_loop(1, N, go, 0)
        pltpu.make_async_copy(
            sbuf.at[slot, me], rbuf.at[slot, me], local_sem.at[slot]
        ).start()

    def arrived(slot):
        def go(k, _):
            frm = lax.rem(me + k, N)
            pltpu.make_async_remote_copy(
                src_ref=sbuf.at[slot, frm],
                dst_ref=rbuf.at[slot, frm],
                send_sem=send_sem.at[slot, frm],
                recv_sem=recv_sem.at[slot, frm],
                device_id={"seq": frm},
                device_id_type=MESH,
            ).wait()
            return 0

        pltpu.make_async_copy(
            sbuf.at[slot, me], rbuf.at[slot, me], local_sem.at[slot]
        ).wait()
        lax.fori_loop(1, N, go, 0)

    gg[0:TOK, :] = (og[...].astype(f32) * up[...].astype(f32)).astype(bf16)
    for i in range(4):
        put(0, i, turned(block(gg, 2 * i)), turned(block(gg, 2 * i + 1)))
    pl.semaphore_wait(barrier, N - 1)

    halos = [
        (pf, TOK - EDGE, nxt),
        (ps, TOK - EDGE, nxt),
        (pf, 0, prv),
        (ps, 0, prv),
        (og, 0, prv),
        (up, 0, prv),
    ]
    halo_copies = [
        pltpu.make_async_remote_copy(
            src_ref=ref.at[pl.ds(start, EDGE), :],
            dst_ref=halo.at[n],
            send_sem=halo_send.at[n],
            recv_sem=halo_recv.at[n],
            device_id={"seq": to},
            device_id_type=MESH,
        )
        for n, (ref, start, to) in enumerate(halos)
    ]
    for copy in halo_copies:
        copy.start()
    exchange(0)

    for half in range(2):
        for p in range(2):
            put(
                1,
                2 * half + p,
                flipped(block(fr, 2 * (3 - 2 * p) + half)),
                flipped(block(fr, 2 * (2 - 2 * p) + half)),
            )
    exchange(1)

    for copy in halo_copies:
        copy.wait()
    before = me > 0
    after = me < N - 1
    for x, src, n in ((pfx, pf, 0), (psx, ps, 1)):
        x[0:EDGE, :] = jnp.where(before, halo[n].astype(f32), 0.0)
        x[EDGE : EDGE + TOK, :] = src[...].astype(f32)
        x[EDGE + TOK :, :] = halo[n + 2].astype(f32)
    gg[TOK:, :] = jnp.where(after, halo[4].astype(f32) * halo[5].astype(f32), 0.0).astype(bf16)
    for x, w, dst in ((pfx, c1, fc), (psx, c2, sc)):
        dst[...] = (
            w[0:1, :] * x[EDGE : EDGE + EXT, :]
            + w[1:2, :] * x[EDGE - 1 : EDGE - 1 + EXT, :]
            + w[2:3, :] * x[EDGE - 2 : EDGE - 2 + EXT, :]
        )

    def prod(i):
        return (block(fc, i) * block(sc, i)).astype(bf16)

    for half in range(2):
        for p in range(2):
            put(
                2,
                2 * half + p,
                flipped(prod(2 * (3 - 2 * p) + half)),
                flipped(prod(2 * (2 - 2 * p) + half)),
            )
    exchange(2)

    frp[...] = jnp.zeros_like(frp)
    gin[BLOCKS:, :, :] = jnp.zeros((gin.shape[0] - BLOCKS, OWN, LANES), f32)
    y[0, 64, :, :, :] = jnp.zeros((2, OWN, LANES), f32)

    arrived(0)
    gin[0:BLOCKS, :, :] = rbuf[0].astype(f32).reshape(BLOCKS, OWN, LANES)
    for slot in (1, 2):
        arrived(slot)

        def unpack(s, _, slot=slot):
            rows = rbuf[slot, N - 1 - s].astype(f32).reshape(2, 4, OWN, LANES)
            fin[slot - 1, :, pl.ds(4 * s, 4), :, :] = rows
            return 0

        lax.fori_loop(0, N, unpack, 0)

    mask = col <= row

    def rolled(jj, ch):
        line = gin[jj, pl.ds(ch, 1), :]
        return pltpu.roll(
            jnp.broadcast_to(line, (LANES, LANES)), 1, 1, stride=1, stride_axis=0
        )

    def channel(ch, _):
        for f in range(2):
            for h in range(2):
                frp[f, h, 0:64, :] = fin[f, h, :, ch, :]

        def shift(r, _):
            for f in range(2):
                for h in range(2):
                    ls[r, f, :, h * LANES : (h + 1) * LANES] = frp[
                        f, h, pl.ds(r, 112), :
                    ].astype(bf16)
            return 0

        lax.fori_loop(0, 16, shift, 0)
        r1 = rolled(1, ch)
        h0 = jnp.where(mask, rolled(0, ch), r1).astype(bf16)
        acc[...] = jnp.zeros_like(acc)
        for group in range(4):
            rows = 16 * (group + 1)
            tot = jnp.zeros((2 * rows, 2 * LANES), f32)
            for k in range(16):
                j = 16 * group + k
                r2 = rolled(2 * j + 2, ch)
                r3 = rolled(2 * j + 3, ch)
                h1 = jnp.where(mask, r1, r2).astype(bf16)
                h2 = jnp.where(mask, r2, r3).astype(bf16)
                rhs = jnp.concatenate(
                    [jnp.concatenate([h0, h1], 1), jnp.concatenate([h1, h2], 1)], 0
                )
                top = 16 * (3 - group)
                lhs = ls[15 - k, :, top : top + rows, :].reshape(2 * rows, 2 * LANES)
                tot += jnp.dot(lhs, rhs, preferred_element_type=f32)
                r1, h0 = r3, h2
            acc[:, 0:rows, :] += tot.reshape(2, rows, 2 * LANES)
        for f in range(2):
            for h in range(2):
                y[f, 0:64, h, ch, :] = acc[f, :, h * LANES : (h + 1) * LANES]
        return 0

    lax.fori_loop(0, OWN, channel, 0)

    ybuf[0] = y[0].reshape(65 * 2 * OWN, LANES).astype(bf16)
    ybuf[1, 0:1024, :] = (
        y[1, 0:64].reshape(1024, LANES) * (TOK * N) ** -0.5
    ).astype(bf16)

    def home(f, to, frm):
        dst, size = ((rmix, 80), (rcor, 64))[f]
        return ybuf.at[f, pl.ds(pl.multiple_of(64 * to, 64), size), :], dst.at[frm]

    def back(k, _):
        to = lax.rem(me + k, N)
        for f in range(2):
            src, dst = home(f, to, me)
            pltpu.make_async_remote_copy(
                src_ref=src,
                dst_ref=dst,
                send_sem=send_sem.at[3 + f, to],
                recv_sem=recv_sem.at[3 + f, me],
                device_id={"seq": to},
                device_id_type=MESH,
            ).start()
        return 0

    def back_done(k, _):
        frm = lax.rem(me + k, N)
        for f in range(2):
            src, dst = home(f, frm, frm)
            pltpu.make_async_remote_copy(
                src_ref=src,
                dst_ref=dst,
                send_sem=send_sem.at[3 + f, frm],
                recv_sem=recv_sem.at[3 + f, frm],
                device_id={"seq": frm},
                device_id_type=MESH,
            ).wait()
        return 0

    lax.fori_loop(1, N, back, 0)
    for f in range(2):
        src, dst = home(f, me, me)
        pltpu.make_async_copy(src, dst, local_sem.at[3 + f]).start()
    for f in range(2):
        src, dst = home(f, me, me)
        pltpu.make_async_copy(src, dst, local_sem.at[3 + f]).wait()
    lax.fori_loop(1, N, back_done, 0)

    def columns(ref, pair):
        both = ref[:, 16 * pair : 16 * pair + 16, :].astype(f32)
        both = both.reshape(N, 2, OWN, LANES)
        return [jnp.transpose(both[:, n].reshape(LANES, LANES)) for n in range(2)]

    skip = sk[...]

    def grads(start, size, mix):
        at = pl.ds(start, size)
        total = mix + skip * gg[at, :].astype(f32)
        fg[at, :] = (total * sc[at, :]).astype(bf16).astype(f32)
        sg[at, :] = (total * fc[at, :]).astype(bf16).astype(f32)

    for pair in range(4):
        one, two = columns(rmix, pair)
        grads(256 * pair, LANES, one)
        grads(256 * pair + LANES, LANES, two)
        one, two = columns(rcor, pair)
        out_filter[256 * pair : 256 * pair + LANES, :] = one
        out_filter[256 * pair + LANES : 256 * pair + 256, :] = two
    grads(TOK, EXT - TOK, columns(rmix, 4)[0][0 : EXT - TOK])
    for x, w, dst in ((fg, c1, out_first), (sg, c2, out_second)):
        dst[...] = (
            w[0:1, :] * x[0:TOK, :]
            + w[1:2, :] * x[1 : TOK + 1, :]
            + w[2:3, :] * x[2 : TOK + 2, :]
        ).astype(bf16)


def body(pf, ps, og, up, fr, c1, c2, sk):
    vmem = pl.BlockSpec(memory_space=pltpu.VMEM)
    dma = pltpu.SemaphoreType.DMA
    return pl.pallas_call(
        kernel,
        out_shape=(
            jax.ShapeDtypeStruct((TOK, LANES), bf16),
            jax.ShapeDtypeStruct((TOK, LANES), bf16),
            jax.ShapeDtypeStruct((TOK, LANES), f32),
        ),
        in_specs=[vmem] * 8,
        out_specs=(vmem,) * 3,
        scratch_shapes=[
            pltpu.VMEM((6, EDGE, LANES), bf16),
            pltpu.VMEM((3, N, 64, LANES), bf16),
            pltpu.VMEM((3, N, 64, LANES), bf16),
            pltpu.VMEM((2, 1040, LANES), bf16),
            pltpu.VMEM((N, 80, LANES), bf16),
            pltpu.VMEM((N, 64, LANES), bf16),
            pltpu.VMEM((EDGE + EXT, LANES), f32),
            pltpu.VMEM((EDGE + EXT, LANES), f32),
            pltpu.VMEM((EXT, LANES), f32),
            pltpu.VMEM((EXT, LANES), f32),
            pltpu.VMEM((EXT, LANES), bf16),
            pltpu.VMEM((EXT, LANES), f32),
            pltpu.VMEM((EXT, LANES), f32),
            pltpu.VMEM((BLOCKS + 2, OWN, LANES), f32),
            pltpu.VMEM((2, 2, 64, OWN, LANES), f32),
            pltpu.VMEM((2, 2, 128, LANES), f32),
            pltpu.VMEM((16, 2, 112, 2 * LANES), bf16),
            pltpu.VMEM((2, 64, 2 * LANES), f32),
            pltpu.VMEM((2, 65, 2, OWN, LANES), f32),
            dma((6,)),
            dma((6,)),
            dma((5, N)),
            dma((5, N)),
            dma((5,)),
        ],
        compiler_params=pltpu.CompilerParams(
            collective_id=0, has_side_effects=True, vmem_limit_bytes=48 * 2**20
        ),
        cost_estimate=pl.CostEstimate(
            flops=2 * 4 * 10**9, bytes_accessed=3 * 10**6, transcendentals=0
        ),
    )(pf, ps, og, up, fr, c1, c2, sk.reshape(1, LANES))


def solution(mesh):
    tok = P("seq", "ch")
    return jax.shard_map(
        body,
        mesh=mesh,
        in_specs=(tok,) * 5 + (P(None, "ch"), P(None, "ch"), P("ch")),
        out_specs=(tok,) * 3,
        check_vma=False,
    )
```

```python
from functools import partial

import jax
import jax.numpy as jnp
from jax import lax
from jax.experimental import pallas as pl
from jax.experimental.pallas import tpu as pltpu
from jax.sharding import PartitionSpec as P

f32 = jnp.float32
bf16 = jnp.bfloat16
MESH = pl.DeviceIdType.MESH
N = 16
LANES = 128
TOK = 1024
EXT = TOK + 16
OWN = 8
BLOCKS = 128
EDGE = 16


def rows_of(block):
    return pl.ds(pl.multiple_of(block, 16), 16)


def kernel(
    pf_in, ps_in, og_in, up_in, fr_in, c1_in, c2_in, sk_in,
    out_first, out_second, out_filter,
    pf, ps, og, up, fr, c1, c2, sk,
    halo, sbuf, rbuf, ybuf, rmix, rcor,
    pfx, psx, fc, sc, gg, fg, sg,
    gin, fin, frp, ls, acc, y,
    halo_send, halo_recv, send_sem, recv_sem, local_sem, in_sem,
):
    me = lax.axis_index("seq")
    nxt = lax.rem(me + 1, N)
    prv = lax.rem(me + N - 1, N)

    barrier = pltpu.get_barrier_semaphore()

    def greet(k, _):
        pl.semaphore_signal(
            barrier, inc=1, device_id={"seq": lax.rem(me + k, N)}, device_id_type=MESH
        )
        return 0

    lax.fori_loop(1, N, greet, 0)

    fetched = [
        pltpu.make_async_copy(src, dst, in_sem.at[n])
        for n, (src, dst) in enumerate(
            (
                (og_in, og),
                (up_in, up),
                (fr_in, fr),
                (pf_in, pf),
                (ps_in, ps),
                (c1_in, c1),
                (c2_in, c2),
                (sk_in, sk),
            )
        )
    ]
    for copy in fetched:
        copy.start()

    row = lax.broadcasted_iota(jnp.int32, (LANES, LANES), 0)
    col = lax.broadcasted_iota(jnp.int32, (LANES, LANES), 1)
    eye = (row == col).astype(f32).astype(bf16)
    flip = (row + col == LANES - 1).astype(f32).astype(bf16)

    def turned(block):
        return lax.dot_general(
            eye, block, (((1,), (1,)), ((), ())), preferred_element_type=f32
        )

    def flipped(block):
        back = jnp.dot(flip, block, preferred_element_type=f32).astype(bf16)
        return turned(back)

    def put(slot, pair, one, two):
        both = jnp.concatenate(
            [one.reshape(N, OWN, LANES), two.reshape(N, OWN, LANES)], axis=1
        )
        sbuf[slot, :, 16 * pair : 16 * pair + 16, :] = both.astype(bf16)

    def block(ref, i):
        return ref[LANES * i : LANES * (i + 1), :]

    def exchange(slot):
        def go(k, _):
            to = lax.rem(me + k, N)
            pltpu.make_async_remote_copy(
                src_ref=sbuf.at[slot, to],
                dst_ref=rbuf.at[slot, me],
                send_sem=send_sem.at[slot, to],
                recv_sem=recv_sem.at[slot, me],
                device_id={"seq": to},
                device_id_type=MESH,
            ).start()
            return 0

        lax.fori_loop(1, N, go, 0)
        pltpu.make_async_copy(
            sbuf.at[slot, me], rbuf.at[slot, me], local_sem.at[slot]
        ).start()

    def arrived(slot):
        def go(k, _):
            frm = lax.rem(me + k, N)
            pltpu.make_async_remote_copy(
                src_ref=sbuf.at[slot, frm],
                dst_ref=rbuf.at[slot, frm],
                send_sem=send_sem.at[slot, frm],
                recv_sem=recv_sem.at[slot, frm],
                device_id={"seq": frm},
                device_id_type=MESH,
            ).wait()
            return 0

        pltpu.make_async_copy(
            sbuf.at[slot, me], rbuf.at[slot, me], local_sem.at[slot]
        ).wait()
        lax.fori_loop(1, N, go, 0)

    fetched[0].wait()
    fetched[1].wait()
    gg[0:TOK, :] = (og[...].astype(f32) * up[...].astype(f32)).astype(bf16)
    for i in range(4):
        put(0, i, turned(block(gg, 2 * i)), turned(block(gg, 2 * i + 1)))
    pl.semaphore_wait(barrier, N - 1)

    halos = [
        (pf_in, TOK - EDGE, nxt),
        (ps_in, TOK - EDGE, nxt),
        (pf_in, 0, prv),
        (ps_in, 0, prv),
        (og_in, 0, prv),
        (up_in, 0, prv),
    ]
    halo_copies = [
        pltpu.make_async_remote_copy(
            src_ref=ref.at[pl.ds(start, EDGE), :],
            dst_ref=halo.at[n],
            send_sem=halo_send.at[n],
            recv_sem=halo_recv.at[n],
            device_id={"seq": to},
            device_id_type=MESH,
        )
        for n, (ref, start, to) in enumerate(halos)
    ]
    for copy in halo_copies:
        copy.start()
    exchange(0)

    fetched[2].wait()
    for half in range(2):
        for p in range(2):
            put(
                1,
                2 * half + p,
                flipped(block(fr, 2 * (3 - 2 * p) + half)),
                flipped(block(fr, 2 * (2 - 2 * p) + half)),
            )
    exchange(1)

    for copy in fetched[3:]:
        copy.wait()
    for copy in halo_copies:
        copy.wait()
    before = me > 0
    after = me < N - 1
    for x, src, n in ((pfx, pf, 0), (psx, ps, 1)):
        x[0:EDGE, :] = jnp.where(before, halo[n].astype(f32), 0.0)
        x[EDGE : EDGE + TOK, :] = src[...].astype(f32)
        x[EDGE + TOK :, :] = halo[n + 2].astype(f32)
    gg[TOK:, :] = jnp.where(after, halo[4].astype(f32) * halo[5].astype(f32), 0.0).astype(bf16)
    for x, w, dst in ((pfx, c1, fc), (psx, c2, sc)):
        dst[...] = (
            w[0:1, :] * x[EDGE : EDGE + EXT, :]
            + w[1:2, :] * x[EDGE - 1 : EDGE - 1 + EXT, :]
            + w[2:3, :] * x[EDGE - 2 : EDGE - 2 + EXT, :]
        )

    def prod(i):
        return (block(fc, i) * block(sc, i)).astype(bf16)

    for half in range(2):
        for p in range(2):
            put(
                2,
                2 * half + p,
                flipped(prod(2 * (3 - 2 * p) + half)),
                flipped(prod(2 * (2 - 2 * p) + half)),
            )
    exchange(2)

    frp[...] = jnp.zeros_like(frp)
    gin[BLOCKS:, :, :] = jnp.zeros((gin.shape[0] - BLOCKS, OWN, LANES), f32)
    y[0, 64, :, :, :] = jnp.zeros((2, OWN, LANES), f32)

    arrived(0)
    gin[0:BLOCKS, :, :] = rbuf[0].astype(f32).reshape(BLOCKS, OWN, LANES)
    for slot in (1, 2):
        arrived(slot)

        def unpack(s, _, slot=slot):
            rows = rbuf[slot, N - 1 - s].astype(f32).reshape(2, 4, OWN, LANES)
            fin[slot - 1, :, pl.ds(4 * s, 4), :, :] = rows
            return 0

        lax.fori_loop(0, N, unpack, 0)

    mask = col <= row

    def rolled(jj, ch):
        line = gin[jj, pl.ds(ch, 1), :]
        return pltpu.roll(
            jnp.broadcast_to(line, (LANES, LANES)), 1, 1, stride=1, stride_axis=0
        )

    def channel(ch, _):
        for f in range(2):
            for h in range(2):
                frp[f, h, 0:64, :] = fin[f, h, :, ch, :]

        def shift(r, _):
            for f in range(2):
                for h in range(2):
                    ls[r, f, h] = frp[f, h, pl.ds(r, 112), :].astype(bf16)
            return 0

        lax.fori_loop(0, 16, shift, 0, unroll=True)
        r1 = rolled(1, ch)
        h0 = jnp.where(mask, rolled(0, ch), r1).astype(bf16)
        acc[...] = jnp.zeros_like(acc)
        for group in range(4):
            rows = 16 * (group + 1)
            left, right = [], []
            for k in range(16):
                j = 16 * group + k
                r2 = rolled(2 * j + 2, ch)
                r3 = rolled(2 * j + 3, ch)
                h1 = jnp.where(mask, r1, r2).astype(bf16)
                h2 = jnp.where(mask, r2, r3).astype(bf16)
                right += [jnp.concatenate([h0, h1], 1), jnp.concatenate([h1, h2], 1)]
                top = 16 * (3 - group)
                for h in range(2):
                    left.append(ls[15 - k, :, h, top : top + rows, :].reshape(2 * rows, LANES))
                r1, h0 = r3, h2
            tot = jnp.dot(
                jnp.concatenate(left, 1),
                jnp.concatenate(right, 0),
                preferred_element_type=f32,
            )
            acc[:, 0:rows, :] += tot.reshape(2, rows, 2 * LANES)
        for f in range(2):
            for h in range(2):
                y[f, 0:64, h, ch, :] = acc[f, :, h * LANES : (h + 1) * LANES]
        return 0

    lax.fori_loop(0, OWN, channel, 0)

    ybuf[0] = y[0].reshape(65 * 2 * OWN, LANES).astype(bf16)
    ybuf[1, 0:1024, :] = (
        y[1, 0:64].reshape(1024, LANES) * (TOK * N) ** -0.5
    ).astype(bf16)

    def home(f, to, frm):
        dst, size = ((rmix, 80), (rcor, 64))[f]
        return ybuf.at[f, pl.ds(pl.multiple_of(64 * to, 64), size), :], dst.at[frm]

    def back(k, _):
        to = lax.rem(me + k, N)
        for f in range(2):
            src, dst = home(f, to, me)
            pltpu.make_async_remote_copy(
                src_ref=src,
                dst_ref=dst,
                send_sem=send_sem.at[3 + f, to],
                recv_sem=recv_sem.at[3 + f, me],
                device_id={"seq": to},
                device_id_type=MESH,
            ).start()
        return 0

    def back_done(k, _):
        frm = lax.rem(me + k, N)
        for f in range(2):
            src, dst = home(f, frm, frm)
            pltpu.make_async_remote_copy(
                src_ref=src,
                dst_ref=dst,
                send_sem=send_sem.at[3 + f, frm],
                recv_sem=recv_sem.at[3 + f, frm],
                device_id={"seq": frm},
                device_id_type=MESH,
            ).wait()
        return 0

    lax.fori_loop(1, N, back, 0)
    for f in range(2):
        src, dst = home(f, me, me)
        pltpu.make_async_copy(src, dst, local_sem.at[3 + f]).start()
    for f in range(2):
        src, dst = home(f, me, me)
        pltpu.make_async_copy(src, dst, local_sem.at[3 + f]).wait()
    lax.fori_loop(1, N, back_done, 0)

    def columns(ref, pair):
        both = ref[:, 16 * pair : 16 * pair + 16, :].astype(f32)
        both = both.reshape(N, 2, OWN, LANES)
        return [jnp.transpose(both[:, n].reshape(LANES, LANES)) for n in range(2)]

    skip = sk[...]

    def grads(start, size, mix):
        at = pl.ds(start, size)
        total = mix + skip * gg[at, :].astype(f32)
        fg[at, :] = (total * sc[at, :]).astype(bf16).astype(f32)
        sg[at, :] = (total * fc[at, :]).astype(bf16).astype(f32)

    for pair in range(4):
        one, two = columns(rmix, pair)
        grads(256 * pair, LANES, one)
        grads(256 * pair + LANES, LANES, two)
        one, two = columns(rcor, pair)
        out_filter[256 * pair : 256 * pair + LANES, :] = one
        out_filter[256 * pair + LANES : 256 * pair + 256, :] = two
    grads(TOK, EXT - TOK, columns(rmix, 4)[0][0 : EXT - TOK])
    for x, w, dst in ((fg, c1, out_first), (sg, c2, out_second)):
        dst[...] = (
            w[0:1, :] * x[0:TOK, :]
            + w[1:2, :] * x[1 : TOK + 1, :]
            + w[2:3, :] * x[2 : TOK + 2, :]
        ).astype(bf16)


def body(pf, ps, og, up, fr, c1, c2, sk):
    vmem = pl.BlockSpec(memory_space=pltpu.VMEM)
    dma = pltpu.SemaphoreType.DMA
    return pl.pallas_call(
        kernel,
        out_shape=(
            jax.ShapeDtypeStruct((TOK, LANES), bf16),
            jax.ShapeDtypeStruct((TOK, LANES), bf16),
            jax.ShapeDtypeStruct((TOK, LANES), f32),
        ),
        in_specs=[pl.BlockSpec(memory_space=pltpu.HBM)] * 8,
        out_specs=(vmem,) * 3,
        scratch_shapes=[
            *[pltpu.VMEM((TOK, LANES), bf16)] * 5,
            *[pltpu.VMEM((3, LANES), f32)] * 2,
            pltpu.VMEM((1, LANES), f32),
            pltpu.VMEM((6, EDGE, LANES), bf16),
            pltpu.VMEM((3, N, 64, LANES), bf16),
            pltpu.VMEM((3, N, 64, LANES), bf16),
            pltpu.VMEM((2, 1040, LANES), bf16),
            pltpu.VMEM((N, 80, LANES), bf16),
            pltpu.VMEM((N, 64, LANES), bf16),
            pltpu.VMEM((EDGE + EXT, LANES), f32),
            pltpu.VMEM((EDGE + EXT, LANES), f32),
            pltpu.VMEM((EXT, LANES), f32),
            pltpu.VMEM((EXT, LANES), f32),
            pltpu.VMEM((EXT, LANES), bf16),
            pltpu.VMEM((EXT, LANES), f32),
            pltpu.VMEM((EXT, LANES), f32),
            pltpu.VMEM((BLOCKS + 2, OWN, LANES), f32),
            pltpu.VMEM((2, 2, 64, OWN, LANES), f32),
            pltpu.VMEM((2, 2, 128, LANES), f32),
            pltpu.VMEM((16, 2, 2, 112, LANES), bf16),
            pltpu.VMEM((2, 64, 2 * LANES), f32),
            pltpu.VMEM((2, 65, 2, OWN, LANES), f32),
            dma((6,)),
            dma((6,)),
            dma((5, N)),
            dma((5, N)),
            dma((5,)),
            dma((8,)),
        ],
        compiler_params=pltpu.CompilerParams(
            collective_id=0, has_side_effects=True, vmem_limit_bytes=56 * 2**20
        ),
        cost_estimate=pl.CostEstimate(
            flops=2 * 4 * 10**9, bytes_accessed=3 * 10**6, transcendentals=0
        ),
    )(pf, ps, og, up, fr, c1, c2, sk.reshape(1, LANES))


def solution(mesh):
    tok = P("seq", "ch")
    return jax.shard_map(
        body,
        mesh=mesh,
        in_specs=(tok,) * 5 + (P(None, "ch"), P(None, "ch"), P("ch")),
        out_specs=(tok,) * 3,
        check_vma=False,
    )
```

```python
from functools import partial

import jax
import jax.numpy as jnp
from jax import lax
from jax.experimental import pallas as pl
from jax.experimental.pallas import tpu as pltpu
from jax.sharding import PartitionSpec as P

f32 = jnp.float32
bf16 = jnp.bfloat16
MESH = pl.DeviceIdType.MESH
N = 16
LANES = 128
TOK = 1024
EXT = TOK + 16
OWN = 8
EDGE = 16


def kernel(
    pf_in, ps_in, og_in, up_in, fr_in, c1_in, c2_in, sk_in,
    out_first, out_second, out_filter,
    pf, ps, og, up, fr, c1, c2, sk,
    halo, sbuf, rbuf, ybuf, rret, tok,
    pfx, psx, fc, sc, gg, fg, sg,
    gin, fin, frp, ls, acc, y,
    halo_send, halo_recv, send_sem, recv_sem, local_sem, in_sem,
):
    me = lax.axis_index("seq")
    nxt = lax.rem(me + 1, N)
    prv = lax.rem(me + N - 1, N)

    barrier = pltpu.get_barrier_semaphore()

    def greet(k, _):
        pl.semaphore_signal(
            barrier, inc=1, device_id={"seq": lax.rem(me + k, N)}, device_id_type=MESH
        )
        return 0

    lax.fori_loop(1, N, greet, 0)

    fetched = [
        pltpu.make_async_copy(src, dst, in_sem.at[n])
        for n, (src, dst) in enumerate(
            (
                (og_in, og),
                (up_in, up),
                (fr_in, fr),
                (pf_in, pf),
                (ps_in, ps),
                (c1_in, c1),
                (c2_in, c2),
                (sk_in, sk),
            )
        )
    ]
    for copy in fetched:
        copy.start()

    row = lax.broadcasted_iota(jnp.int32, (LANES, LANES), 0)
    col = lax.broadcasted_iota(jnp.int32, (LANES, LANES), 1)
    flip = (row + col == LANES - 1).astype(f32).astype(bf16)
    row2 = lax.broadcasted_iota(jnp.int32, (256, 256), 0)
    col2 = lax.broadcasted_iota(jnp.int32, (256, 256), 1)
    picked = ((row2 & 4) << 5) + (row2 & 120) + ((row2 >> 7) << 2) + (row2 & 3)
    pick = (picked == col2).astype(f32).astype(bf16)

    def put(base, blocks):
        pairs = [jnp.concatenate(blocks[2 * q : 2 * q + 2], axis=1) for q in range(4)]
        turned = lax.dot_general(
            pick,
            jnp.concatenate(pairs, axis=0),
            (((1,), (1,)), ((), ())),
            preferred_element_type=f32,
        )
        for n in range(2):
            both = jnp.concatenate(
                [
                    turned[:, LANES * q : LANES * (q + 1)].reshape(2, N, OWN, LANES)
                    for q in (2 * n, 2 * n + 1)
                ],
                axis=2,
            ).astype(bf16)
            for half in range(2):
                sbuf[half, :, base + 16 * n : base + 16 * n + 16, :] = both[half]

    def backwards(blocks):
        wide = jnp.concatenate([blocks[6 - (n & 6) + (n & 1)] for n in range(8)], axis=1)
        back = jnp.dot(flip, wide, preferred_element_type=f32).astype(bf16)
        return [back[:, LANES * n : LANES * (n + 1)] for n in range(8)]

    def blocks_of(ref):
        return [ref[LANES * i : LANES * (i + 1), :] for i in range(8)]

    messages = ((0, 0, 64), (0, 64, 32), (1, 0, 96))

    def exchange(m):
        half, start, size = messages[m]
        part = pl.ds(start, size)

        def go(k, _):
            to = lax.rem(me + k, N)
            pltpu.make_async_remote_copy(
                src_ref=sbuf.at[half, to, part],
                dst_ref=rbuf.at[half, me, part],
                send_sem=send_sem.at[m, to],
                recv_sem=recv_sem.at[m, me],
                device_id={"seq": to},
                device_id_type=MESH,
            ).start()
            return 0

        lax.fori_loop(1, N, go, 0)
        pltpu.make_async_copy(
            sbuf.at[half, me, part], rbuf.at[half, me, part], local_sem.at[m]
        ).start()

    def arrived(m):
        half, start, size = messages[m]
        part = pl.ds(start, size)

        def go(k, _):
            frm = lax.rem(me + k, N)
            pltpu.make_async_remote_copy(
                src_ref=sbuf.at[half, frm, part],
                dst_ref=rbuf.at[half, frm, part],
                send_sem=send_sem.at[m, frm],
                recv_sem=recv_sem.at[m, frm],
                device_id={"seq": frm},
                device_id_type=MESH,
            ).wait()
            return 0

        pltpu.make_async_copy(
            sbuf.at[half, me, part], rbuf.at[half, me, part], local_sem.at[m]
        ).wait()
        lax.fori_loop(1, N, go, 0)

    fetched[0].wait()
    fetched[1].wait()
    gg[0:TOK, :] = (og[...].astype(f32) * up[...].astype(f32)).astype(bf16)
    put(0, blocks_of(gg))
    fetched[2].wait()
    put(32, backwards(blocks_of(fr)))
    pl.semaphore_wait(barrier, N - 1)

    halos = [
        (pf_in, TOK - EDGE, nxt),
        (ps_in, TOK - EDGE, nxt),
        (pf_in, 0, prv),
        (ps_in, 0, prv),
        (og_in, 0, prv),
        (up_in, 0, prv),
    ]
    halo_copies = [
        pltpu.make_async_remote_copy(
            src_ref=ref.at[pl.ds(start, EDGE), :],
            dst_ref=halo.at[n],
            send_sem=halo_send.at[n],
            recv_sem=halo_recv.at[n],
            device_id={"seq": to},
            device_id_type=MESH,
        )
        for n, (ref, start, to) in enumerate(halos)
    ]
    for copy in halo_copies:
        copy.start()
    exchange(0)

    for copy in fetched[3:]:
        copy.wait()
    for copy in halo_copies:
        copy.wait()
    before = me > 0
    after = me < N - 1
    for x, src, n in ((pfx, pf, 0), (psx, ps, 1)):
        x[0:EDGE, :] = jnp.where(before, halo[n].astype(f32), 0.0)
        x[EDGE : EDGE + TOK, :] = src[...].astype(f32)
        x[EDGE + TOK :, :] = halo[n + 2].astype(f32)
    gg[TOK:, :] = jnp.where(after, halo[4].astype(f32) * halo[5].astype(f32), 0.0).astype(bf16)
    for x, w, dst in ((pfx, c1, fc), (psx, c2, sc)):
        dst[...] = (
            w[0:1, :] * x[EDGE : EDGE + EXT, :]
            + w[1:2, :] * x[EDGE - 1 : EDGE - 1 + EXT, :]
            + w[2:3, :] * x[EDGE - 2 : EDGE - 2 + EXT, :]
        )

    put(64, backwards([(f * g).astype(bf16) for f, g in zip(blocks_of(fc), blocks_of(sc))]))
    exchange(1)
    exchange(2)

    frp[...] = jnp.zeros_like(frp)
    gin[64:, :, :] = jnp.zeros((2, OWN, LANES), f32)
    y[64, :, :, :] = jnp.zeros((2, OWN, LANES), f32)

    def unpack_gated(half):
        rows = rbuf[half, :, 0:32, :].astype(f32)
        gin[0:64, :, :] = rows.reshape(64, OWN, LANES)

    def unpack_filter(half, f):
        for s in range(N):
            rows = rbuf[half, N - 1 - s, 32 * f + 32 : 32 * f + 64, :].astype(f32)
            fin[f, 4 * s : 4 * s + 4, :, :] = rows.reshape(4, OWN, LANES)

    mask = col <= row

    def rolled(jj, ch):
        line = gin[jj // 2, pl.ds(4 * (jj % 2) + ch, 1), :]
        return pltpu.roll(
            jnp.broadcast_to(line, (LANES, LANES)), 1, 1, stride=1, stride_axis=0
        )

    def channel(ch, _):
        for f in range(2):
            for h in range(2):
                frp[f, h, 0:64, :] = fin[f, :, 4 * h + ch, :]

        def shift(r, _):
            for f in range(2):
                for h in range(2):
                    ls[r, f, h] = frp[f, h, pl.ds(r, 112), :].astype(bf16)
            return 0

        lax.fori_loop(0, 16, shift, 0, unroll=True)
        r1 = rolled(1, ch)
        h0 = jnp.where(mask, rolled(0, ch), r1).astype(bf16)
        acc[...] = jnp.zeros_like(acc)
        for group in range(4):
            rows = 16 * (group + 1)
            left, right = [], []
            for k in range(16):
                j = 16 * group + k
                r2 = rolled(2 * j + 2, ch)
                r3 = rolled(2 * j + 3, ch)
                h1 = jnp.where(mask, r1, r2).astype(bf16)
                h2 = jnp.where(mask, r2, r3).astype(bf16)
                right += [jnp.concatenate([h0, h1], 1), jnp.concatenate([h1, h2], 1)]
                top = 16 * (3 - group)
                for h in range(2):
                    left.append(ls[15 - k, :, h, top : top + rows, :].reshape(2 * rows, LANES))
                r1, h0 = r3, h2
            tot = jnp.dot(
                jnp.concatenate(left, 1),
                jnp.concatenate(right, 0),
                preferred_element_type=f32,
            )
            acc[:, 0:rows, :] += tot.reshape(2, rows, 2 * LANES)
        for f in range(2):
            for h in range(2):
                y[0:64, h, 4 * f + ch, :] = (
                    acc[f, :, h * LANES : (h + 1) * LANES] * (1.0, (TOK * N) ** -0.5)[f]
                )
        return 0

    def home(half, to, frm):
        rows = pl.ds(pl.multiple_of(64 * to, 64), 80)
        return ybuf.at[half, rows, :], rret.at[half, frm]

    def back(half):
        def go(k, _):
            to = lax.rem(me + k, N)
            src, dst = home(half, to, me)
            pltpu.make_async_remote_copy(
                src_ref=src,
                dst_ref=dst,
                send_sem=send_sem.at[3 + half, to],
                recv_sem=recv_sem.at[3 + half, me],
                device_id={"seq": to},
                device_id_type=MESH,
            ).start()
            return 0

        ybuf[half] = y[...].reshape(65 * 2 * OWN, LANES).astype(bf16)
        lax.fori_loop(1, N, go, 0)
        src, dst = home(half, me, me)
        pltpu.make_async_copy(src, dst, local_sem.at[3 + half]).start()

    def back_done(half):
        def go(k, _):
            frm = lax.rem(me + k, N)
            src, dst = home(half, frm, frm)
            pltpu.make_async_remote_copy(
                src_ref=src,
                dst_ref=dst,
                send_sem=send_sem.at[3 + half, frm],
                recv_sem=recv_sem.at[3 + half, frm],
                device_id={"seq": frm},
                device_id_type=MESH,
            ).wait()
            return 0

        src, dst = home(half, me, me)
        pltpu.make_async_copy(src, dst, local_sem.at[3 + half]).wait()
        lax.fori_loop(1, N, go, 0)

    arrived(0)
    unpack_gated(0)
    unpack_filter(0, 0)
    arrived(1)
    unpack_filter(0, 1)
    lax.fori_loop(0, 4, channel, 0)
    back(0)
    arrived(2)
    unpack_gated(1)
    unpack_filter(1, 0)
    unpack_filter(1, 1)
    lax.fori_loop(0, 4, channel, 0)
    back(1)

    def columns(half, pair):
        both = rret[half, :, 16 * pair : 16 * pair + 16, :].astype(f32)
        both = both.reshape(N, 2, OWN, LANES)
        for n in range(2):
            turned = jnp.transpose(both[:, n].reshape(LANES, LANES))
            at = LANES * (2 * pair + n)
            tok[half, at : at + LANES, :] = turned.astype(bf16)

    skip = sk[...]

    def grads(start, size, mix):
        at = pl.ds(start, size)
        total = mix + skip * gg[at, :].astype(f32)
        fg[at, :] = (total * sc[at, :]).astype(bf16).astype(f32)
        sg[at, :] = (total * fc[at, :]).astype(bf16).astype(f32)

    for half in range(2):
        back_done(half)
        for pair in range(5):
            columns(half, pair)
    for i in range(9):
        size = LANES if i < 8 else EXT - TOK
        at = pl.ds(LANES * i, size)
        both = jnp.dot(
            jnp.concatenate([tok[0, at, :], tok[1, at, :]], axis=1),
            pick,
            preferred_element_type=f32,
        )
        grads(LANES * i, size, both[:, 0:LANES])
        if i < 8:
            out_filter[at, :] = both[:, LANES:]
    for x, w, dst in ((fg, c1, out_first), (sg, c2, out_second)):
        dst[...] = (
            w[0:1, :] * x[0:TOK, :]
            + w[1:2, :] * x[1 : TOK + 1, :]
            + w[2:3, :] * x[2 : TOK + 2, :]
        ).astype(bf16)


def body(pf, ps, og, up, fr, c1, c2, sk):
    vmem = pl.BlockSpec(memory_space=pltpu.VMEM)
    dma = pltpu.SemaphoreType.DMA
    return pl.pallas_call(
        kernel,
        out_shape=(
            jax.ShapeDtypeStruct((TOK, LANES), bf16),
            jax.ShapeDtypeStruct((TOK, LANES), bf16),
            jax.ShapeDtypeStruct((TOK, LANES), f32),
        ),
        in_specs=[pl.BlockSpec(memory_space=pltpu.HBM)] * 8,
        out_specs=(vmem,) * 3,
        scratch_shapes=[
            *[pltpu.VMEM((TOK, LANES), bf16)] * 5,
            *[pltpu.VMEM((3, LANES), f32)] * 2,
            pltpu.VMEM((1, LANES), f32),
            pltpu.VMEM((6, EDGE, LANES), bf16),
            pltpu.VMEM((2, N, 96, LANES), bf16),
            pltpu.VMEM((2, N, 96, LANES), bf16),
            pltpu.VMEM((2, 1040, LANES), bf16),
            pltpu.VMEM((2, N, 80, LANES), bf16),
            pltpu.VMEM((2, 10 * LANES, LANES), bf16),
            pltpu.VMEM((EDGE + EXT, LANES), f32),
            pltpu.VMEM((EDGE + EXT, LANES), f32),
            pltpu.VMEM((EXT, LANES), f32),
            pltpu.VMEM((EXT, LANES), f32),
            pltpu.VMEM((EXT, LANES), bf16),
            pltpu.VMEM((EXT, LANES), f32),
            pltpu.VMEM((EXT, LANES), f32),
            pltpu.VMEM((66, OWN, LANES), f32),
            pltpu.VMEM((2, 64, OWN, LANES), f32),
            pltpu.VMEM((2, 2, 128, LANES), f32),
            pltpu.VMEM((16, 2, 2, 112, LANES), bf16),
            pltpu.VMEM((2, 64, 2 * LANES), f32),
            pltpu.VMEM((65, 2, OWN, LANES), f32),
            dma((6,)),
            dma((6,)),
            dma((5, N)),
            dma((5, N)),
            dma((5,)),
            dma((8,)),
        ],
        compiler_params=pltpu.CompilerParams(
            collective_id=0, has_side_effects=True, vmem_limit_bytes=56 * 2**20
        ),
        cost_estimate=pl.CostEstimate(
            flops=2 * 4 * 10**9, bytes_accessed=3 * 10**6, transcendentals=0
        ),
    )(pf, ps, og, up, fr, c1, c2, sk.reshape(1, LANES))


def solution(mesh):
    tok = P("seq", "ch")
    return jax.shard_map(
        body,
        mesh=mesh,
        in_specs=(tok,) * 5 + (P(None, "ch"), P(None, "ch"), P("ch")),
        out_specs=(tok,) * 3,
        check_vma=False,
    )
```

```python
from functools import partial

import jax
import jax.numpy as jnp
from jax import lax
from jax.experimental import pallas as pl
from jax.experimental.pallas import tpu as pltpu
from jax.sharding import PartitionSpec as P

f32 = jnp.float32
bf16 = jnp.bfloat16
MESH = pl.DeviceIdType.MESH
N = 16
LANES = 128
TOK = 1024
EXT = TOK + 16
OWN = 8
EDGE = 16


def kernel(
    pf_in, ps_in, og_in, up_in, fr_in, c1_in, c2_in, sk_in,
    out_first, out_second, out_filter,
    pf, ps, og, up, fr, c1, c2, sk,
    halo, sbuf, rbuf, ybuf, rret, tok,
    pfx, psx, fc, sc, gg, fg, sg,
    gin, fin, frp, ls, acc, y,
    halo_send, halo_recv, send_sem, recv_sem, local_sem, in_sem,
):
    me = lax.axis_index("seq")
    nxt = lax.rem(me + 1, N)
    prv = lax.rem(me + N - 1, N)

    barrier = pltpu.get_barrier_semaphore()

    def greet(k, _):
        pl.semaphore_signal(
            barrier, inc=1, device_id={"seq": lax.rem(me + k, N)}, device_id_type=MESH
        )
        return 0

    lax.fori_loop(1, N, greet, 0)

    fetched = [
        pltpu.make_async_copy(src, dst, in_sem.at[n])
        for n, (src, dst) in enumerate(
            (
                (og_in, og),
                (up_in, up),
                (fr_in, fr),
                (pf_in, pf),
                (ps_in, ps),
                (c1_in, c1),
                (c2_in, c2),
                (sk_in, sk),
            )
        )
    ]
    for copy in fetched:
        copy.start()

    row2 = lax.broadcasted_iota(jnp.int32, (256, 256), 0)
    col2 = lax.broadcasted_iota(jnp.int32, (256, 256), 1)
    picked = ((row2 & 4) << 5) + (row2 & 120) + ((row2 >> 7) << 2) + (row2 & 3)
    pick = (picked == col2).astype(f32).astype(bf16)
    source = ((row2 & 64) << 1) + ((row2 >> 7) << 6) + 63 - (row2 & 63)
    flip = (source == col2).astype(f32).astype(bf16)

    def put(base, blocks):
        pairs = [jnp.concatenate(blocks[2 * q : 2 * q + 2], axis=1) for q in range(4)]
        turned = lax.dot_general(
            pick,
            jnp.concatenate(pairs, axis=0),
            (((1,), (1,)), ((), ())),
            preferred_element_type=f32,
        )
        for n in range(2):
            both = jnp.concatenate(
                [
                    turned[:, LANES * q : LANES * (q + 1)].reshape(2, N, OWN, LANES)
                    for q in (2 * n, 2 * n + 1)
                ],
                axis=2,
            ).astype(bf16)
            for half in range(2):
                sbuf[half, :, base + 16 * n : base + 16 * n + 16, :] = both[half]

    def backwards(quarters):
        wide = jnp.concatenate(quarters[::-1], axis=1)
        back = jnp.dot(flip, wide, preferred_element_type=f32).astype(bf16)
        return [
            back[LANES * z : LANES * (z + 1), LANES * q : LANES * (q + 1)]
            for q in range(4)
            for z in range(2)
        ]

    def blocks_of(ref, size):
        return [ref[size * i : size * (i + 1), :] for i in range(TOK // size)]

    messages = ((0, 0, 64), (0, 64, 32), (1, 0, 96))

    def exchange(m):
        half, start, size = messages[m]
        part = pl.ds(start, size)

        def go(k, _):
            to = lax.rem(me + k, N)
            pltpu.make_async_remote_copy(
                src_ref=sbuf.at[half, to, part],
                dst_ref=rbuf.at[half, me, part],
                send_sem=send_sem.at[m, to],
                recv_sem=recv_sem.at[m, me],
                device_id={"seq": to},
                device_id_type=MESH,
            ).start()
            return 0

        lax.fori_loop(1, N, go, 0)
        pltpu.make_async_copy(
            sbuf.at[half, me, part], rbuf.at[half, me, part], local_sem.at[m]
        ).start()

    def arrived(m):
        half, start, size = messages[m]
        part = pl.ds(start, size)

        def go(k, _):
            frm = lax.rem(me + k, N)
            pltpu.make_async_remote_copy(
                src_ref=sbuf.at[half, frm, part],
                dst_ref=rbuf.at[half, frm, part],
                send_sem=send_sem.at[m, frm],
                recv_sem=recv_sem.at[m, frm],
                device_id={"seq": frm},
                device_id_type=MESH,
            ).wait()
            return 0

        pltpu.make_async_copy(
            sbuf.at[half, me, part], rbuf.at[half, me, part], local_sem.at[m]
        ).wait()
        lax.fori_loop(1, N, go, 0)

    pl.semaphore_wait(barrier, N - 1)

    halos = [
        (pf_in, TOK - EDGE, nxt),
        (ps_in, TOK - EDGE, nxt),
        (pf_in, 0, prv),
        (ps_in, 0, prv),
        (og_in, 0, prv),
        (up_in, 0, prv),
    ]
    halo_copies = [
        pltpu.make_async_remote_copy(
            src_ref=ref.at[pl.ds(start, EDGE), :],
            dst_ref=halo.at[n],
            send_sem=halo_send.at[n],
            recv_sem=halo_recv.at[n],
            device_id={"seq": to},
            device_id_type=MESH,
        )
        for n, (ref, start, to) in enumerate(halos)
    ]
    for copy in halo_copies:
        copy.start()

    fetched[0].wait()
    fetched[1].wait()
    gg[0:TOK, :] = (og[...].astype(f32) * up[...].astype(f32)).astype(bf16)
    put(0, blocks_of(gg, LANES))
    fetched[2].wait()
    put(32, backwards(blocks_of(fr, 256)))
    exchange(0)

    for copy in fetched[3:]:
        copy.wait()
    for copy in halo_copies:
        copy.wait()
    before = me > 0
    after = me < N - 1
    for x, src, n in ((pfx, pf, 0), (psx, ps, 1)):
        x[0:EDGE, :] = jnp.where(before, halo[n].astype(f32), 0.0)
        x[EDGE : EDGE + TOK, :] = src[...].astype(f32)
        x[EDGE + TOK :, :] = halo[n + 2].astype(f32)
    gg[TOK:, :] = jnp.where(after, halo[4].astype(f32) * halo[5].astype(f32), 0.0).astype(bf16)
    for x, w, dst in ((pfx, c1, fc), (psx, c2, sc)):
        dst[...] = (
            w[0:1, :] * x[EDGE : EDGE + EXT, :]
            + w[1:2, :] * x[EDGE - 1 : EDGE - 1 + EXT, :]
            + w[2:3, :] * x[EDGE - 2 : EDGE - 2 + EXT, :]
        )

    short = zip(blocks_of(fc, 256), blocks_of(sc, 256))
    put(64, backwards([(f * g).astype(bf16) for f, g in short]))
    exchange(1)

    frp[...] = jnp.zeros_like(frp)
    gin[64:, :, :] = jnp.zeros((2, OWN, LANES), f32)
    y[64, :, :, :] = jnp.zeros((2, OWN, LANES), f32)

    def unpack_gated(half):
        rows = rbuf[half, :, 0:32, :].astype(f32)
        gin[0:64, :, :] = rows.reshape(64, OWN, LANES)

    def unpack_filter(half, f):
        for s in range(N):
            rows = rbuf[half, N - 1 - s, 32 * f + 32 : 32 * f + 64, :].astype(f32)
            fin[f, 4 * s : 4 * s + 4, :, :] = rows.reshape(4, OWN, LANES)

    row = lax.broadcasted_iota(jnp.int32, (64, LANES), 0)
    col = lax.broadcasted_iota(jnp.int32, (64, LANES), 1)
    mask = col - row <= 64
    low = col < 64

    def rolled(jj, ch):
        line = gin[jj // 2, pl.ds(4 * (jj % 2) + ch, 1), :]
        return pltpu.roll(
            jnp.broadcast_to(line, (64, LANES)), 65, 1, stride=1, stride_axis=0
        )

    def channel(ch, _):
        for z in range(2):
            for f in range(2):
                frp[z, f, 0:64, :] = fin[f, :, 4 * z + ch, :]
        for r in range(16):
            for z in range(2):
                for f in range(2):
                    ls[r, z, f] = frp[z, f, pl.ds(r, 112), :].astype(bf16)
        acc[...] = jnp.zeros_like(acc)
        lines = [rolled(0, ch)]
        hankel = []

        def more_blocks(count):
            while len(hankel) < count:
                lines.append(rolled(min(len(lines), 128), ch))
                hankel.append(jnp.where(mask, lines[-2], lines[-1]).astype(bf16))

        for group in range(4):
            rows = 16 * (group + 1)
            top = 16 * (3 - group)
            left, right = [], []
            for k in range(16):
                j = 16 * group + k
                left.append(ls[15 - k, :, :, top : top + rows, :].reshape(4 * rows, LANES))
                more_blocks(2 * j + 4)
                for n in (2 * j, 2 * j + 1):
                    right.append(jnp.concatenate(hankel[n : n + 3], axis=1))
            left = jnp.concatenate(left, axis=1)
            right = jnp.concatenate(right, axis=0)
            both = jnp.dot(left, right[:, 0:256], preferred_element_type=f32)
            more = jnp.dot(left[2 * rows :], right[:, 256:], preferred_element_type=f32)
            acc[:, :, 0:rows, 0:256] += both.reshape(2, 2, rows, 256)
            acc[1, :, 0:rows, 256:] += more.reshape(2, rows, LANES)
        for f in range(2):
            moved = [
                pltpu.roll(acc[1, f, :, LANES * n : LANES * (n + 1)], 64, 1)
                for n in range(3)
            ]
            for h in range(2):
                total = acc[0, f, :, LANES * h : LANES * (h + 1)] + jnp.where(
                    low, moved[h], moved[h + 1]
                )
                y[0:64, h, 4 * f + ch, :] = total * (1.0, (TOK * N) ** -0.5)[f]
        return 0

    def home(half, to, frm):
        rows = pl.ds(pl.multiple_of(64 * to, 64), 80)
        return ybuf.at[half, rows, :], rret.at[half, frm]

    def back(half):
        def go(k, _):
            to = lax.rem(me + k, N)
            src, dst = home(half, to, me)
            pltpu.make_async_remote_copy(
                src_ref=src,
                dst_ref=dst,
                send_sem=send_sem.at[3 + half, to],
                recv_sem=recv_sem.at[3 + half, me],
                device_id={"seq": to},
                device_id_type=MESH,
            ).start()
            return 0

        ybuf[half] = y[...].reshape(65 * 2 * OWN, LANES).astype(bf16)
        lax.fori_loop(1, N, go, 0)
        src, dst = home(half, me, me)
        pltpu.make_async_copy(src, dst, local_sem.at[3 + half]).start()

    def back_done(half):
        def go(k, _):
            frm = lax.rem(me + k, N)
            src, dst = home(half, frm, frm)
            pltpu.make_async_remote_copy(
                src_ref=src,
                dst_ref=dst,
                send_sem=send_sem.at[3 + half, frm],
                recv_sem=recv_sem.at[3 + half, frm],
                device_id={"seq": frm},
                device_id_type=MESH,
            ).wait()
            return 0

        src, dst = home(half, me, me)
        pltpu.make_async_copy(src, dst, local_sem.at[3 + half]).wait()
        lax.fori_loop(1, N, go, 0)

    arrived(0)
    unpack_gated(0)
    unpack_filter(0, 0)
    arrived(1)
    exchange(2)
    unpack_filter(0, 1)
    lax.fori_loop(0, 4, channel, 0)
    back(0)
    arrived(2)
    unpack_gated(1)
    unpack_filter(1, 0)
    unpack_filter(1, 1)
    lax.fori_loop(0, 4, channel, 0)
    back(1)

    def columns(half, pair):
        both = rret[half, :, 16 * pair : 16 * pair + 16, :].astype(f32)
        both = both.reshape(N, 2, OWN, LANES)
        for n in range(2):
            turned = jnp.transpose(both[:, n].reshape(LANES, LANES))
            at = LANES * (2 * pair + n)
            tok[half, at : at + LANES, :] = turned.astype(bf16)

    skip = sk[...]

    def grads(start, size, mix):
        at = pl.ds(start, size)
        total = mix + skip * gg[at, :].astype(f32)
        fg[at, :] = (total * sc[at, :]).astype(bf16).astype(f32)
        sg[at, :] = (total * fc[at, :]).astype(bf16).astype(f32)

    for half in range(2):
        back_done(half)
        for pair in range(5):
            columns(half, pair)
    for i in range(9):
        size = LANES if i < 8 else EXT - TOK
        at = pl.ds(LANES * i, size)
        both = jnp.dot(
            jnp.concatenate([tok[0, at, :], tok[1, at, :]], axis=1),
            pick,
            preferred_element_type=f32,
        )
        grads(LANES * i, size, both[:, 0:LANES])
        if i < 8:
            out_filter[at, :] = both[:, LANES:]
    for x, w, dst in ((fg, c1, out_first), (sg, c2, out_second)):
        dst[...] = (
            w[0:1, :] * x[0:TOK, :]
            + w[1:2, :] * x[1 : TOK + 1, :]
            + w[2:3, :] * x[2 : TOK + 2, :]
        ).astype(bf16)


def body(pf, ps, og, up, fr, c1, c2, sk):
    vmem = pl.BlockSpec(memory_space=pltpu.VMEM)
    dma = pltpu.SemaphoreType.DMA
    return pl.pallas_call(
        kernel,
        out_shape=(
            jax.ShapeDtypeStruct((TOK, LANES), bf16),
            jax.ShapeDtypeStruct((TOK, LANES), bf16),
            jax.ShapeDtypeStruct((TOK, LANES), f32),
        ),
        in_specs=[pl.BlockSpec(memory_space=pltpu.HBM)] * 8,
        out_specs=(vmem,) * 3,
        scratch_shapes=[
            *[pltpu.VMEM((TOK, LANES), bf16)] * 5,
            *[pltpu.VMEM((3, LANES), f32)] * 2,
            pltpu.VMEM((1, LANES), f32),
            pltpu.VMEM((6, EDGE, LANES), bf16),
            pltpu.VMEM((2, N, 96, LANES), bf16),
            pltpu.VMEM((2, N, 96, LANES), bf16),
            pltpu.VMEM((2, 1040, LANES), bf16),
            pltpu.VMEM((2, N, 80, LANES), bf16),
            pltpu.VMEM((2, 10 * LANES, LANES), bf16),
            pltpu.VMEM((EDGE + EXT, LANES), f32),
            pltpu.VMEM((EDGE + EXT, LANES), f32),
            pltpu.VMEM((EXT, LANES), f32),
            pltpu.VMEM((EXT, LANES), f32),
            pltpu.VMEM((EXT, LANES), bf16),
            pltpu.VMEM((EXT, LANES), f32),
            pltpu.VMEM((EXT, LANES), f32),
            pltpu.VMEM((66, OWN, LANES), f32),
            pltpu.VMEM((2, 64, OWN, LANES), f32),
            pltpu.VMEM((2, 2, 128, LANES), f32),
            pltpu.VMEM((16, 2, 2, 112, LANES), bf16),
            pltpu.VMEM((2, 2, 64, 3 * LANES), f32),
            pltpu.VMEM((65, 2, OWN, LANES), f32),
            dma((6,)),
            dma((6,)),
            dma((5, N)),
            dma((5, N)),
            dma((5,)),
            dma((8,)),
        ],
        compiler_params=pltpu.CompilerParams(
            collective_id=0, has_side_effects=True, vmem_limit_bytes=56 * 2**20
        ),
        cost_estimate=pl.CostEstimate(
            flops=2 * 4 * 10**9, bytes_accessed=3 * 10**6, transcendentals=0
        ),
    )(pf, ps, og, up, fr, c1, c2, sk.reshape(1, LANES))


def solution(mesh):
    tok = P("seq", "ch")
    return jax.shard_map(
        body,
        mesh=mesh,
        in_specs=(tok,) * 5 + (P(None, "ch"), P(None, "ch"), P("ch")),
        out_specs=(tok,) * 3,
        check_vma=False,
    )
```

```python
from functools import partial

import jax
import jax.numpy as jnp
from jax import lax
from jax.experimental import pallas as pl
from jax.experimental.pallas import tpu as pltpu
from jax.sharding import PartitionSpec as P

f32 = jnp.float32
bf16 = jnp.bfloat16
MESH = pl.DeviceIdType.MESH
N = 16
LANES = 128
TOK = 1024
EXT = TOK + 16
OWN = 8
CHUNKS = 4
ROWS = 64
HOME = 48
EDGE = 16


PARTNERS = sorted(
    ((x, z, c) for x in range(2) for z in range(4) for c in range(2) if x + z + c),
    key=lambda k: -2 * k[0] - min(k[1], 4 - k[1]),
)


def partner(me, k):
    x = lax.rem(me // 8 + k[0], 2)
    z = lax.rem(lax.rem(me // 2, 4) + k[1], 4)
    return 8 * x + 2 * z + lax.rem(lax.rem(me, 2) + k[2], 2)


def kernel(
    pf_in, ps_in, og_in, up_in, fr_in, c1_in, c2_in, sk_in,
    out_first, out_second, out_filter,
    v_first, v_second, v_filter,
    pf, ps, og, up, fr, c1, c2, sk,
    halo, sbuf, rbuf, ybuf, rret, tok, pick,
    pfx, psx, fc, sc, gg, fg, sg,
    gin, fin, frp, ls, acc, y,
    halo_send, halo_recv, send_sem, recv_sem, local_sem, in_sem, out_sem,
):
    me = lax.axis_index("seq")
    nxt = lax.rem(me + 1, N)
    prv = lax.rem(me + N - 1, N)

    barrier = pltpu.get_barrier_semaphore()

    def greet(k, _):
        pl.semaphore_signal(
            barrier, inc=1, device_id={"seq": lax.rem(me + k, N)}, device_id_type=MESH
        )
        return 0

    lax.fori_loop(1, N, greet, 0)

    fetched = [
        pltpu.make_async_copy(src, dst, in_sem.at[n])
        for n, (src, dst) in enumerate(
            (
                (og_in, og),
                (up_in, up),
                (fr_in, fr),
                (pf_in, pf),
                (ps_in, ps),
                (c1_in, c1),
                (c2_in, c2),
                (sk_in, sk),
            )
        )
    ]
    for copy in fetched:
        copy.start()

    row2 = lax.broadcasted_iota(jnp.int32, (512, 512), 0)
    col2 = lax.broadcasted_iota(jnp.int32, (512, 512), 1)
    picked = ((row2 & 6) << 6) + (row2 & 120) + ((row2 >> 7) << 1) + (row2 & 1)
    pick[...] = (picked == col2).astype(f32).astype(bf16)
    row1 = lax.broadcasted_iota(jnp.int32, (256, 256), 0)
    col1 = lax.broadcasted_iota(jnp.int32, (256, 256), 1)
    source = ((row1 & 64) << 1) + ((row1 >> 7) << 6) + 63 - (row1 & 63)
    flip = (source == col1).astype(f32).astype(bf16)

    def put(base, pairs):
        wide = [jnp.concatenate(pairs[n : n + 2], axis=1) for n in (0, 2)]
        turned = lax.dot_general(
            pick[...],
            jnp.concatenate(wide, axis=0),
            (((1,), (1,)), ((), ())),
            preferred_element_type=f32,
        )
        both = jnp.concatenate(
            [
                turned[:, LANES * n : LANES * (n + 1)].reshape(CHUNKS, N, OWN, LANES)
                for n in range(2)
            ],
            axis=2,
        ).astype(bf16)
        for chunk in range(CHUNKS):
            sbuf[chunk, :, base : base + 16, :] = both[chunk]

    def backwards(quarters):
        wide = jnp.concatenate(quarters[::-1], axis=1)
        back = jnp.dot(flip, wide, preferred_element_type=f32).astype(bf16)
        return [
            jnp.concatenate(
                [
                    back[LANES * z : LANES * (z + 1), LANES * q : LANES * (q + 1)]
                    for z in range(2)
                ],
                axis=1,
            )
            for q in range(len(quarters))
        ]

    def paired(blocks):
        return [jnp.concatenate(blocks[n : n + 2], axis=1) for n in range(0, len(blocks), 2)]

    def blocks_of(ref, size):
        return [ref[size * i : size * (i + 1), :] for i in range(TOK // size)]

    partners = [partner(me, k) for k in PARTNERS]

    def exchange(chunk):
        for to in partners:
            pltpu.make_async_remote_copy(
                src_ref=sbuf.at[chunk, to],
                dst_ref=rbuf.at[chunk, me],
                send_sem=send_sem.at[chunk, to],
                recv_sem=recv_sem.at[chunk, me],
                device_id={"seq": to},
                device_id_type=MESH,
            ).start()
        pltpu.make_async_copy(
            sbuf.at[chunk, me], rbuf.at[chunk, me], local_sem.at[chunk]
        ).start()

    def arrived(chunk):
        def go(k, _):
            frm = lax.rem(me + k, N)
            pltpu.make_async_remote_copy(
                src_ref=sbuf.at[chunk, frm],
                dst_ref=rbuf.at[chunk, frm],
                send_sem=send_sem.at[chunk, frm],
                recv_sem=recv_sem.at[chunk, frm],
                device_id={"seq": frm},
                device_id_type=MESH,
            ).wait()
            return 0

        pltpu.make_async_copy(
            sbuf.at[chunk, me], rbuf.at[chunk, me], local_sem.at[chunk]
        ).wait()
        lax.fori_loop(1, N, go, 0)

    fetched[0].wait()
    fetched[1].wait()
    gg[0:TOK, :] = (og[...].astype(f32) * up[...].astype(f32)).astype(bf16)
    put(0, paired(blocks_of(gg, LANES)))
    fetched[2].wait()
    put(16, backwards(blocks_of(fr, 256)))

    for copy in fetched[3:]:
        copy.wait()

    def convolve(start, size):
        for x, w, dst in ((pfx, c1, fc), (psx, c2, sc)):
            dst[start : start + size, :] = (
                w[0:1, :] * x[EDGE + start : EDGE + start + size, :]
                + w[1:2, :] * x[EDGE + start - 1 : EDGE + start - 1 + size, :]
                + w[2:3, :] * x[EDGE + start - 2 : EDGE + start - 2 + size, :]
            )

    def products(quarters):
        return [
            (fc[256 * q : 256 * (q + 1), :] * sc[256 * q : 256 * (q + 1), :]).astype(bf16)
            for q in quarters
        ]

    for x, src in ((pfx, pf), (psx, ps)):
        x[EDGE : EDGE + TOK, :] = src[...].astype(f32)
    for x in (pfx, psx):
        x[0:EDGE, :] = jnp.zeros((EDGE, LANES), f32)
    convolve(0, TOK)
    put(32, backwards(products(range(4))))
    row3 = lax.broadcasted_iota(jnp.int32, (LANES, 2 * EDGE), 0)
    col3 = lax.broadcasted_iota(jnp.int32, (LANES, 2 * EDGE), 1)
    head = (row3 + col3 == 63) & (col3 < 2)
    tail = (row3 - col3 == 127 - 31) & (col3 >= 30)
    edge_pick = (head | tail).astype(f32).astype(bf16)
    edges = jnp.concatenate(
        [
            jnp.dot(
                edge_pick,
                jnp.concatenate([x[0:EDGE, :], x[TOK - EDGE : TOK, :]], axis=0),
                preferred_element_type=f32,
            ).astype(bf16)
            for x in (pf, ps)
        ],
        axis=1,
    )
    put(48, [edges] * 4)

    pl.semaphore_wait(barrier, N - 1)

    halos = [
        (pf_in, TOK - EDGE, nxt),
        (ps_in, TOK - EDGE, nxt),
        (pf_in, 0, prv),
        (ps_in, 0, prv),
        (og_in, 0, prv),
        (up_in, 0, prv),
    ]
    halo_copies = [
        pltpu.make_async_remote_copy(
            src_ref=ref.at[pl.ds(start, EDGE), :],
            dst_ref=halo.at[n],
            send_sem=halo_send.at[n],
            recv_sem=halo_recv.at[n],
            device_id={"seq": to},
            device_id_type=MESH,
        )
        for n, (ref, start, to) in enumerate(halos)
    ]
    for copy in halo_copies:
        copy.start()

    exchange(0)
    exchange(1)

    frp[...] = jnp.zeros_like(frp)
    gin[32] = jnp.zeros((OWN, LANES), f32)
    y[64:] = jnp.zeros((2, OWN, LANES), f32)

    def unpack_gated(chunk):
        rows = rbuf[chunk, :, 0:16, :].astype(f32)
        gin[0:32, :, :] = rows.reshape(32, OWN, LANES)

    lane = lax.broadcasted_iota(jnp.int32, (OWN, LANES), 1)
    place = lax.broadcasted_iota(jnp.int32, (OWN, LANES), 0)

    def taps(chunk):
        mine = OWN * me + 2 * chunk + (place & 1)
        for k in range(3):
            both = jnp.where((place & 2) == 0, c1[k : k + 1, :], c2[k : k + 1, :])
            yield jnp.sum(jnp.where(lane == mine, both, 0.0), axis=1, keepdims=True)

    def unpack_edges(chunk):
        w = list(taps(chunk))
        at63 = lane == 63
        fill = ((place & 6) == 4) & (at63 | (lane == 62))
        last = jnp.zeros((OWN, LANES), f32)
        for s in range(N):
            own = rbuf[chunk, s, 48:64, :].astype(f32)[0:OWN]
            one = jnp.where(at63, last, pltpu.roll(own, LANES - 1, 1))
            two = jnp.where(at63, pltpu.roll(last, 1, 1), pltpu.roll(last, LANES - 1, 1))
            conv = w[0] * own + w[1] * one + w[2] * two
            product = (conv * pltpu.roll(conv, 6, 0)).astype(bf16).astype(f32)
            i = 2 * (N - 1 - s) + 1
            fin[1, i] = jnp.where(fill, product, fin[1, i])
            last = pltpu.roll(own, 64, 1)

    def unpack_filter(chunk, f):
        for s in range(N):
            rows = rbuf[chunk, N - 1 - s, 16 * f + 16 : 16 * f + 32, :].astype(f32)
            fin[f, 2 * s : 2 * s + 2, :, :] = rows.reshape(2, OWN, LANES)

    row = lax.broadcasted_iota(jnp.int32, (64, LANES), 0)
    col = lax.broadcasted_iota(jnp.int32, (64, LANES), 1)
    mask = col - row <= 64
    low = col < 64

    def rolled(jj, ch):
        line = gin[jj // 4, pl.ds(2 * (jj % 4) + ch, 1), :]
        return pltpu.roll(
            jnp.broadcast_to(line, (64, LANES)), 65, 1, stride=1, stride_axis=0
        )

    def channel(ch, _):
        for z in range(2):
            for f in range(2):
                for u in range(2):
                    frp[z, f, pl.ds(u, 32, stride=2), :] = fin[f, :, 4 * u + 2 * z + ch, :]
        for r in range(16):
            for z in range(2):
                for f in range(2):
                    ls[r, z, f] = frp[z, f, pl.ds(r, 112), :].astype(bf16)
        acc[...] = jnp.zeros_like(acc)
        lines = [rolled(0, ch)]
        hankel = []

        def more_blocks(count):
            while len(hankel) < count:
                lines.append(rolled(min(len(lines), 128), ch))
                hankel.append(jnp.where(mask, lines[-2], lines[-1]).astype(bf16))

        for group in range(4):
            rows = 16 * (group + 1)
            top = 16 * (3 - group)
            left, right = [], []
            for k in range(16):
                j = 16 * group + k
                left.append(ls[15 - k, :, :, top : top + rows, :].reshape(4 * rows, LANES))
                more_blocks(2 * j + 4)
                for n in (2 * j, 2 * j + 1):
                    right.append(jnp.concatenate(hankel[n : n + 3], axis=1))
            left = jnp.concatenate(left, axis=1)
            right = jnp.concatenate(right, axis=0)
            both = jnp.dot(left, right[:, 0:256], preferred_element_type=f32)
            more = jnp.dot(left[2 * rows :], right[:, 256:], preferred_element_type=f32)
            acc[:, :, 0:rows, 0:256] += both.reshape(2, 2, rows, 256)
            acc[1, :, 0:rows, 256:] += more.reshape(2, rows, LANES)
        for f in range(2):
            moved = [
                pltpu.roll(acc[1, f, :, LANES * n : LANES * (n + 1)], 64, 1)
                for n in range(3)
            ]
            for h in range(2):
                total = acc[0, f, :, LANES * h : LANES * (h + 1)] + jnp.where(
                    low, moved[h], moved[h + 1]
                )
                y[0:64, 4 * h + 2 * f + ch, :] = total * (1.0, (TOK * N) ** -0.5)[f]
        return 0

    def home(chunk, to, frm):
        rows = pl.ds(pl.multiple_of(32 * to, 32), HOME)
        return ybuf.at[chunk, rows, :], rret.at[chunk, frm]

    def back(chunk):
        ybuf[chunk] = y[...].reshape(66 * OWN, LANES).astype(bf16)
        for to in partners:
            src, dst = home(chunk, to, me)
            pltpu.make_async_remote_copy(
                src_ref=src,
                dst_ref=dst,
                send_sem=send_sem.at[CHUNKS + chunk, to],
                recv_sem=recv_sem.at[CHUNKS + chunk, me],
                device_id={"seq": to},
                device_id_type=MESH,
            ).start()
        src, dst = home(chunk, me, me)
        pltpu.make_async_copy(src, dst, local_sem.at[CHUNKS + chunk]).start()

    def back_done(chunk):
        def go(k, _):
            frm = lax.rem(me + k, N)
            src, dst = home(chunk, frm, frm)
            pltpu.make_async_remote_copy(
                src_ref=src,
                dst_ref=dst,
                send_sem=send_sem.at[CHUNKS + chunk, frm],
                recv_sem=recv_sem.at[CHUNKS + chunk, frm],
                device_id={"seq": frm},
                device_id_type=MESH,
            ).wait()
            return 0

        src, dst = home(chunk, me, me)
        pltpu.make_async_copy(src, dst, local_sem.at[CHUNKS + chunk]).wait()
        lax.fori_loop(1, N, go, 0)

    def one_chunk(chunk, _):
        arrived(chunk)

        @pl.when(chunk < CHUNKS - 2)
        def _():
            exchange(chunk + 2)

        unpack_gated(chunk)
        unpack_filter(chunk, 0)
        unpack_filter(chunk, 1)
        unpack_edges(chunk)
        lax.fori_loop(0, 2, channel, 0)
        back(chunk)
        return 0

    lax.fori_loop(0, CHUNKS, one_chunk, 0)

    for copy in halo_copies:
        copy.wait()
    before = me > 0
    after = me < N - 1
    for n, x in enumerate((pfx, psx)):
        x[0:EDGE, :] = jnp.where(before, halo[n].astype(f32), 0.0)
        x[EDGE + TOK :, :] = halo[n + 2].astype(f32)
    convolve(0, EDGE)
    convolve(TOK, EXT - TOK)
    gg[TOK:, :] = jnp.where(after, halo[4].astype(f32) * halo[5].astype(f32), 0.0).astype(bf16)

    def columns(chunk, pair):
        both = rret[chunk, :, 16 * pair : 16 * pair + 16, :].astype(f32)
        both = both.reshape(N, 2, OWN, LANES)
        for n in range(2):
            turned = jnp.transpose(both[:, n].reshape(LANES, LANES))
            tok[chunk, 2 * pair + n] = turned.astype(bf16)

    skip = sk[...]

    def grads(start, size, mix):
        at = pl.ds(start, size)
        total = mix + skip * gg[at, :].astype(f32)
        fg[at, :] = (total * sc[at, :]).astype(bf16).astype(f32)
        sg[at, :] = (total * fc[at, :]).astype(bf16).astype(f32)

    for chunk in range(CHUNKS):
        back_done(chunk)
        for pair in range(3):
            columns(chunk, pair)
    for i in range(5):
        both = jnp.dot(
            jnp.concatenate([tok[chunk, i] for chunk in range(CHUNKS)], axis=1),
            pick[...],
            preferred_element_type=f32,
        )
        if i == 4:
            grads(TOK, EXT - TOK, both[0 : EXT - TOK, 0:LANES])
            break
        for h in range(2):
            at = 256 * i + LANES * h
            grads(at, LANES, both[:, 256 * h : 256 * h + LANES])
            v_filter[at : at + LANES, :] = both[:, 256 * h + LANES : 256 * h + 256]
    copies = [
        pltpu.make_async_copy(src, dst, out_sem.at[n])
        for n, (src, dst) in enumerate(
            ((v_filter, out_filter), (v_first, out_first), (v_second, out_second))
        )
    ]
    copies[0].start()
    for x, w, dst, copy in ((fg, c1, v_first, copies[1]), (sg, c2, v_second, copies[2])):
        dst[...] = (
            w[0:1, :] * x[0:TOK, :]
            + w[1:2, :] * x[1 : TOK + 1, :]
            + w[2:3, :] * x[2 : TOK + 2, :]
        ).astype(bf16)
        copy.start()
    for copy in copies:
        copy.wait()


def body(pf, ps, og, up, fr, c1, c2, sk):
    hbm = pl.BlockSpec(memory_space=pltpu.HBM)
    dma = pltpu.SemaphoreType.DMA
    return pl.pallas_call(
        kernel,
        out_shape=(
            jax.ShapeDtypeStruct((TOK, LANES), bf16),
            jax.ShapeDtypeStruct((TOK, LANES), bf16),
            jax.ShapeDtypeStruct((TOK, LANES), f32),
        ),
        in_specs=[hbm] * 8,
        out_specs=(hbm,) * 3,
        scratch_shapes=[
            *[pltpu.VMEM((TOK, LANES), bf16)] * 2,
            pltpu.VMEM((TOK, LANES), f32),
            *[pltpu.VMEM((TOK, LANES), bf16)] * 5,
            *[pltpu.VMEM((3, LANES), f32)] * 2,
            pltpu.VMEM((1, LANES), f32),
            pltpu.VMEM((6, EDGE, LANES), bf16),
            pltpu.VMEM((CHUNKS, N, ROWS, LANES), bf16),
            pltpu.VMEM((CHUNKS, N, ROWS, LANES), bf16),
            pltpu.VMEM((CHUNKS, 66 * OWN, LANES), bf16),
            pltpu.VMEM((CHUNKS, N, HOME, LANES), bf16),
            pltpu.VMEM((CHUNKS, 6, LANES, LANES), bf16),
            pltpu.VMEM((512, 512), bf16),
            pltpu.VMEM((EDGE + EXT, LANES), f32),
            pltpu.VMEM((EDGE + EXT, LANES), f32),
            pltpu.VMEM((EXT, LANES), f32),
            pltpu.VMEM((EXT, LANES), f32),
            pltpu.VMEM((EXT, LANES), bf16),
            pltpu.VMEM((EXT, LANES), f32),
            pltpu.VMEM((EXT, LANES), f32),
            pltpu.VMEM((33, OWN, LANES), f32),
            pltpu.VMEM((2, 32, OWN, LANES), f32),
            pltpu.VMEM((2, 2, 128, LANES), f32),
            pltpu.VMEM((16, 2, 2, 112, LANES), bf16),
            pltpu.VMEM((2, 2, 64, 3 * LANES), f32),
            pltpu.VMEM((66, OWN, LANES), f32),
            dma((6,)),
            dma((6,)),
            dma((2 * CHUNKS, N)),
            dma((2 * CHUNKS, N)),
            dma((2 * CHUNKS,)),
            dma((8,)),
            dma((3,)),
        ],
        compiler_params=pltpu.CompilerParams(
            collective_id=0, has_side_effects=True, vmem_limit_bytes=56 * 2**20
        ),
        cost_estimate=pl.CostEstimate(
            flops=2 * 4 * 10**9, bytes_accessed=3 * 10**6, transcendentals=0
        ),
    )(pf, ps, og, up, fr, c1, c2, sk.reshape(1, LANES))


def solution(mesh):
    tok = P("seq", "ch")
    return jax.shard_map(
        body,
        mesh=mesh,
        in_specs=(tok,) * 5 + (P(None, "ch"), P(None, "ch"), P("ch")),
        out_specs=(tok,) * 3,
        check_vma=False,
    )
```

```python
from functools import partial

import jax
import jax.numpy as jnp
from jax import lax
from jax.experimental import pallas as pl
from jax.experimental.pallas import tpu as pltpu
from jax.sharding import PartitionSpec as P

f32 = jnp.float32
bf16 = jnp.bfloat16
MESH = pl.DeviceIdType.MESH
N = 16
LANES = 128
TOK = 1024
EXT = TOK + 16
OWN = 8
CHUNKS = 4
ROWS = 48
HOME = 32
EDGE = 16


PARTNERS = sorted(
    ((x, z, c) for x in range(2) for z in range(4) for c in range(2) if x + z + c),
    key=lambda k: -2 * k[0] - min(k[1], 4 - k[1]),
)


def partner(me, k):
    x = lax.rem(me // 8 + k[0], 2)
    z = lax.rem(lax.rem(me // 2, 4) + k[1], 4)
    return 8 * x + 2 * z + lax.rem(lax.rem(me, 2) + k[2], 2)


def kernel(
    pf_in, ps_in, og_in, up_in, fr_in, c1_in, c2_in, sk_in,
    out_first, out_second, out_filter,
    v_first, v_second, v_filter,
    pf, ps, og, up, fr, c1, c2, sk,
    halo, sbuf, rbuf, ybuf, rret, tok, pick, ylast, first, heads,
    pfx, psx, fc, sc, gg, fg, sg,
    gin, fin, frp, ls, acc, y,
    halo_send, halo_recv, send_sem, recv_sem, local_sem, in_sem, out_sem,
):
    me = lax.axis_index("seq")
    nxt = lax.rem(me + 1, N)
    prv = lax.rem(me + N - 1, N)

    barrier = pltpu.get_barrier_semaphore()

    def greet(k, _):
        pl.semaphore_signal(
            barrier, inc=1, device_id={"seq": lax.rem(me + k, N)}, device_id_type=MESH
        )
        return 0

    lax.fori_loop(1, N, greet, 0)

    fetched = [
        pltpu.make_async_copy(src, dst, in_sem.at[n])
        for n, (src, dst) in enumerate(
            (
                (og_in, og),
                (up_in, up),
                (fr_in, fr),
                (pf_in, pf),
                (ps_in, ps),
                (c1_in, c1),
                (c2_in, c2),
                (sk_in, sk),
            )
        )
    ]
    for copy in fetched:
        copy.start()

    row2 = lax.broadcasted_iota(jnp.int32, (512, 512), 0)
    col2 = lax.broadcasted_iota(jnp.int32, (512, 512), 1)
    picked = ((row2 & 6) << 6) + (row2 & 120) + ((row2 >> 7) << 1) + (row2 & 1)
    pick[...] = (picked == col2).astype(f32).astype(bf16)
    row1 = lax.broadcasted_iota(jnp.int32, (256, 256), 0)
    col1 = lax.broadcasted_iota(jnp.int32, (256, 256), 1)
    source = ((row1 & 64) << 1) + ((row1 >> 7) << 6) + 63 - (row1 & 63)
    flip = (source == col1).astype(f32).astype(bf16)
    eye = (row1 == col1)[0:LANES, 0:LANES].astype(f32).astype(bf16)

    def put(base, pairs):
        wide = [jnp.concatenate(pairs[n : n + 2], axis=1) for n in (0, 2)]
        turned = lax.dot_general(
            pick[...],
            jnp.concatenate(wide, axis=0),
            (((1,), (1,)), ((), ())),
            preferred_element_type=f32,
        )
        both = jnp.concatenate(
            [
                turned[:, LANES * n : LANES * (n + 1)].reshape(CHUNKS, N, OWN, LANES)
                for n in range(2)
            ],
            axis=2,
        ).astype(bf16)
        for chunk in range(CHUNKS):
            sbuf[chunk, :, base : base + 16, :] = both[chunk]

    def backwards(quarters):
        wide = jnp.concatenate(quarters[::-1], axis=1)
        back = jnp.dot(flip, wide, preferred_element_type=f32).astype(bf16)
        return [
            jnp.concatenate(
                [
                    back[LANES * z : LANES * (z + 1), LANES * q : LANES * (q + 1)]
                    for z in range(2)
                ],
                axis=1,
            )
            for q in range(len(quarters))
        ]

    def paired(blocks):
        return [jnp.concatenate(blocks[n : n + 2], axis=1) for n in range(0, len(blocks), 2)]

    def blocks_of(ref, size):
        return [ref[size * i : size * (i + 1), :] for i in range(TOK // size)]

    partners = [partner(me, k) for k in PARTNERS]

    def sent(chunk, to, frm):
        part = pl.ds(0, ROWS + 16 if isinstance(chunk, int) and chunk == 0 else ROWS)
        return sbuf.at[chunk, to, part], rbuf.at[chunk, frm, part]

    def exchange(chunk):
        for to in partners:
            src, dst = sent(chunk, to, me)
            pltpu.make_async_remote_copy(
                src_ref=src,
                dst_ref=dst,
                send_sem=send_sem.at[chunk, to],
                recv_sem=recv_sem.at[chunk, me],
                device_id={"seq": to},
                device_id_type=MESH,
            ).start()
        src, dst = sent(chunk, me, me)
        pltpu.make_async_copy(src, dst, local_sem.at[chunk]).start()

    def arrived(chunk):
        def go(k, _):
            frm = lax.rem(me + k, N)
            src, dst = sent(chunk, frm, frm)
            pltpu.make_async_remote_copy(
                src_ref=src,
                dst_ref=dst,
                send_sem=send_sem.at[chunk, frm],
                recv_sem=recv_sem.at[chunk, frm],
                device_id={"seq": frm},
                device_id_type=MESH,
            ).wait()
            return 0

        src, dst = sent(chunk, me, me)
        pltpu.make_async_copy(src, dst, local_sem.at[chunk]).wait()
        lax.fori_loop(1, N, go, 0)

    fetched[0].wait()
    fetched[1].wait()
    gg[0:TOK, :] = (og[...].astype(f32) * up[...].astype(f32)).astype(bf16)
    put(0, paired(blocks_of(gg, LANES)))
    fetched[2].wait()
    put(16, backwards(blocks_of(fr, 256)))

    for copy in fetched[3:]:
        copy.wait()

    def convolve(start, size):
        for x, w, dst in ((pfx, c1, fc), (psx, c2, sc)):
            dst[start : start + size, :] = (
                w[0:1, :] * x[EDGE + start : EDGE + start + size, :]
                + w[1:2, :] * x[EDGE + start - 1 : EDGE + start - 1 + size, :]
                + w[2:3, :] * x[EDGE + start - 2 : EDGE + start - 2 + size, :]
            )

    def products(quarters):
        return [
            (fc[256 * q : 256 * (q + 1), :] * sc[256 * q : 256 * (q + 1), :]).astype(bf16)
            for q in quarters
        ]

    for x, src in ((pfx, pf), (psx, ps)):
        x[EDGE : EDGE + TOK, :] = src[...].astype(f32)
    for x in (pfx, psx):
        x[0:EDGE, :] = jnp.zeros((EDGE, LANES), f32)
    convolve(0, TOK)
    put(32, backwards(products(range(4))))
    row3 = lax.broadcasted_iota(jnp.int32, (LANES, 2 * EDGE), 0)
    col3 = lax.broadcasted_iota(jnp.int32, (LANES, 2 * EDGE), 1)
    head = (row3 + col3 == 63) & (col3 < 2)
    tail = (row3 - col3 == 127 - 31) & (col3 >= 30)
    edge_pick = (head | tail).astype(f32).astype(bf16)
    edges = jnp.concatenate(
        [
            jnp.dot(
                edge_pick,
                jnp.concatenate([x[0:EDGE, :], x[TOK - EDGE : TOK, :]], axis=0),
                preferred_element_type=f32,
            ).astype(bf16)
            for x in (pf, ps)
        ],
        axis=0,
    )
    turned = [
        lax.dot_general(
            eye,
            edges[LANES * z : LANES * (z + 1)],
            (((1,), (1,)), ((), ())),
            preferred_element_type=f32,
        ).reshape(N, OWN, LANES)
        for z in range(2)
    ]
    sbuf[0, :, ROWS : ROWS + 16, :] = jnp.concatenate(turned, axis=1).astype(bf16)

    pl.semaphore_wait(barrier, N - 1)

    halos = [
        (pf_in, TOK - EDGE, nxt),
        (ps_in, TOK - EDGE, nxt),
        (pf_in, 0, prv),
        (ps_in, 0, prv),
        (og_in, 0, prv),
        (up_in, 0, prv),
    ]
    halo_copies = [
        pltpu.make_async_remote_copy(
            src_ref=ref.at[pl.ds(start, EDGE), :],
            dst_ref=halo.at[n],
            send_sem=halo_send.at[n],
            recv_sem=halo_recv.at[n],
            device_id={"seq": to},
            device_id_type=MESH,
        )
        for n, (ref, start, to) in enumerate(halos)
    ]
    for copy in halo_copies:
        copy.start()

    for chunk in range(CHUNKS):
        exchange(chunk)

    frp[...] = jnp.zeros_like(frp)
    gin[32] = jnp.zeros((OWN, LANES), f32)
    y[64] = jnp.zeros((OWN, LANES), f32)

    def unpack_gated(chunk):
        rows = rbuf[chunk, :, 0:16, :].astype(f32)
        gin[0:32, :, :] = rows.reshape(32, OWN, LANES)

    lane = lax.broadcasted_iota(jnp.int32, (OWN, LANES), 1)
    place = lax.broadcasted_iota(jnp.int32, (OWN, LANES), 0)

    def taps(ref):
        mine = lane == OWN * me + place
        for k in range(3):
            yield jnp.sum(jnp.where(mine, ref[k : k + 1, :], 0.0), axis=1, keepdims=True)

    def unpack_edges():
        weights = [list(taps(ref)) for ref in (c1, c2)]
        at63 = lane == 63
        last = [jnp.zeros((OWN, LANES), f32)] * 2
        for s in range(N):
            rows = rbuf[0, s, ROWS : ROWS + 16, :].astype(f32)
            conv = []
            for z in range(2):
                own = rows[OWN * z : OWN * (z + 1)]
                w = weights[z]
                one = jnp.where(at63, last[z], pltpu.roll(own, LANES - 1, 1))
                two = jnp.where(
                    at63, pltpu.roll(last[z], 1, 1), pltpu.roll(last[z], LANES - 1, 1)
                )
                conv.append(w[0] * own + w[1] * one + w[2] * two)
                last[z] = pltpu.roll(own, 64, 1)
            first[N - 1 - s] = (conv[0] * conv[1]).astype(bf16).astype(f32)

    def unpack_filter(chunk, f):
        for s in range(N):
            rows = rbuf[chunk, N - 1 - s, 16 * f + 16 : 16 * f + 32, :].astype(f32)
            fin[f, 2 * s : 2 * s + 2, :, :] = rows.reshape(2, OWN, LANES)

    row = lax.broadcasted_iota(jnp.int32, (64, LANES), 0)
    col = lax.broadcasted_iota(jnp.int32, (64, LANES), 1)
    mask = col - row <= 64
    low = col < 64
    fill = ((col == 62) | (col == 63))[0:N]

    def rolled(jj, ch):
        line = gin[jj // 4, pl.ds(2 * (jj % 4) + ch, 1), :]
        return pltpu.roll(
            jnp.broadcast_to(line, (64, LANES)), 65, 1, stride=1, stride_axis=0
        )

    def channel(ch, chunk):
        for z in range(2):
            for f in range(2):
                for u in range(2):
                    frp[z, f, pl.ds(u, 32, stride=2), :] = fin[f, :, 4 * u + 2 * z + ch, :]
        at = pl.ds(3, N, stride=4)
        frp[0, 1, at, :] = jnp.where(
            fill, first[:, 2 * chunk + ch, :], frp[0, 1, at, :]
        )
        for r in range(16):
            for z in range(2):
                for f in range(2):
                    ls[r, z, f] = frp[z, f, pl.ds(r, 112), :].astype(bf16)
        acc[...] = jnp.zeros_like(acc)
        lines = [rolled(0, ch)]
        hankel = []

        def more_blocks(count):
            while len(hankel) < count:
                lines.append(rolled(min(len(lines), 128), ch))
                hankel.append(jnp.where(mask, lines[-2], lines[-1]).astype(bf16))

        for group in range(4):
            rows = 16 * (group + 1)
            top = 16 * (3 - group)
            left, right = [], []
            for k in range(16):
                j = 16 * group + k
                left.append(ls[15 - k, :, :, top : top + rows, :].reshape(4 * rows, LANES))
                more_blocks(2 * j + 4)
                for n in (2 * j, 2 * j + 1):
                    right.append(jnp.concatenate(hankel[n : n + 3], axis=1))
            left = jnp.concatenate(left, axis=1)
            right = jnp.concatenate(right, axis=0)
            both = jnp.dot(left, right[:, 0:256], preferred_element_type=f32)
            more = jnp.dot(left[2 * rows :], right[:, 256:], preferred_element_type=f32)
            acc[:, :, 0:rows, 0:256] += both.reshape(2, 2, rows, 256)
            acc[1, :, 0:rows, 256:] += more.reshape(2, rows, LANES)
        for f in range(2):
            moved = [
                pltpu.roll(acc[1, f, :, LANES * n : LANES * (n + 1)], 64, 1)
                for n in range(3)
            ]
            for h in range(2):
                total = acc[0, f, :, LANES * h : LANES * (h + 1)] + jnp.where(
                    low, moved[h], moved[h + 1]
                )
                y[0:64, 4 * h + 2 * f + ch, :] = total * (1.0, (TOK * N) ** -0.5)[f]
        heads[:, 2 * chunk + ch, :] = y[pl.ds(4, N, stride=4), ch, :]
        return chunk

    def home(chunk, to, frm):
        if isinstance(chunk, int) and chunk == CHUNKS - 1:
            return ylast.at[to], rret.at[chunk, frm]
        rows = pl.ds(pl.multiple_of(HOME * to, HOME), HOME)
        return ybuf.at[chunk, rows, :], rret.at[chunk, frm, pl.ds(0, HOME)]

    def back(chunk):
        for to in partners:
            src, dst = home(chunk, to, me)
            pltpu.make_async_remote_copy(
                src_ref=src,
                dst_ref=dst,
                send_sem=send_sem.at[CHUNKS + chunk, to],
                recv_sem=recv_sem.at[CHUNKS + chunk, me],
                device_id={"seq": to},
                device_id_type=MESH,
            ).start()
        src, dst = home(chunk, me, me)
        pltpu.make_async_copy(src, dst, local_sem.at[CHUNKS + chunk]).start()

    def back_done(chunk):
        def go(k, _):
            frm = lax.rem(me + k, N)
            src, dst = home(chunk, frm, frm)
            pltpu.make_async_remote_copy(
                src_ref=src,
                dst_ref=dst,
                send_sem=send_sem.at[CHUNKS + chunk, frm],
                recv_sem=recv_sem.at[CHUNKS + chunk, frm],
                device_id={"seq": frm},
                device_id_type=MESH,
            ).wait()
            return 0

        src, dst = home(chunk, me, me)
        pltpu.make_async_copy(src, dst, local_sem.at[CHUNKS + chunk]).wait()
        lax.fori_loop(1, N, go, 0)

    def one_chunk(chunk, _):
        @pl.when(chunk > 0)
        def _():
            arrived(chunk)

        unpack_gated(chunk)
        unpack_filter(chunk, 0)
        unpack_filter(chunk, 1)
        lax.fori_loop(0, 2, channel, chunk)

        @pl.when(chunk < CHUNKS - 1)
        def _():
            ybuf[chunk] = y[0:64].reshape(64 * OWN, LANES).astype(bf16)
            back(chunk)

        return 0

    arrived(0)
    unpack_edges()
    lax.fori_loop(0, CHUNKS, one_chunk, 0)
    ylast[:, 0:HOME, :] = y[0:64].reshape(N, HOME, LANES).astype(bf16)
    ylast[:, HOME:, :] = jnp.concatenate([heads[...]] * 2, axis=1).astype(bf16)
    back(CHUNKS - 1)

    for copy in halo_copies:
        copy.wait()
    before = me > 0
    after = me < N - 1
    for n, x in enumerate((pfx, psx)):
        x[0:EDGE, :] = jnp.where(before, halo[n].astype(f32), 0.0)
        x[EDGE + TOK :, :] = halo[n + 2].astype(f32)
    convolve(0, EDGE)
    convolve(TOK, EXT - TOK)
    gg[TOK:, :] = jnp.where(after, halo[4].astype(f32) * halo[5].astype(f32), 0.0).astype(bf16)

    def columns(chunk, pair):
        both = rret[chunk, :, 16 * pair : 16 * pair + 16, :].astype(f32)
        both = both.reshape(N, 2, OWN, LANES)
        for n in range(2):
            turned = jnp.transpose(both[:, n].reshape(LANES, LANES))
            tok[chunk, 2 * pair + n] = turned.astype(bf16)

    skip = sk[...]

    def grads(start, size, mix):
        at = pl.ds(start, size)
        total = mix + skip * gg[at, :].astype(f32)
        fg[at, :] = (total * sc[at, :]).astype(bf16).astype(f32)
        sg[at, :] = (total * fc[at, :]).astype(bf16).astype(f32)

    for chunk in range(CHUNKS):
        back_done(chunk)
        for pair in range(2):
            columns(chunk, pair)
    following = rret[CHUNKS - 1, :, HOME:, :].astype(f32)[:, 0:OWN].reshape(LANES, LANES)
    grads(TOK, EXT - TOK, jnp.transpose(following)[0 : EXT - TOK])
    for i in range(4):
        both = jnp.dot(
            jnp.concatenate([tok[chunk, i] for chunk in range(CHUNKS)], axis=1),
            pick[...],
            preferred_element_type=f32,
        )
        for h in range(2):
            at = 256 * i + LANES * h
            grads(at, LANES, both[:, 256 * h : 256 * h + LANES])
            v_filter[at : at + LANES, :] = both[:, 256 * h + LANES : 256 * h + 256]
    copies = [
        pltpu.make_async_copy(src, dst, out_sem.at[n])
        for n, (src, dst) in enumerate(
            ((v_filter, out_filter), (v_first, out_first), (v_second, out_second))
        )
    ]
    copies[0].start()
    for x, w, dst, copy in ((fg, c1, v_first, copies[1]), (sg, c2, v_second, copies[2])):
        dst[...] = (
            w[0:1, :] * x[0:TOK, :]
            + w[1:2, :] * x[1 : TOK + 1, :]
            + w[2:3, :] * x[2 : TOK + 2, :]
        ).astype(bf16)
        copy.start()
    for copy in copies:
        copy.wait()


def body(pf, ps, og, up, fr, c1, c2, sk):
    hbm = pl.BlockSpec(memory_space=pltpu.HBM)
    dma = pltpu.SemaphoreType.DMA
    return pl.pallas_call(
        kernel,
        out_shape=(
            jax.ShapeDtypeStruct((TOK, LANES), bf16),
            jax.ShapeDtypeStruct((TOK, LANES), bf16),
            jax.ShapeDtypeStruct((TOK, LANES), f32),
        ),
        in_specs=[hbm] * 8,
        out_specs=(hbm,) * 3,
        scratch_shapes=[
            *[pltpu.VMEM((TOK, LANES), bf16)] * 2,
            pltpu.VMEM((TOK, LANES), f32),
            *[pltpu.VMEM((TOK, LANES), bf16)] * 5,
            *[pltpu.VMEM((3, LANES), f32)] * 2,
            pltpu.VMEM((1, LANES), f32),
            pltpu.VMEM((6, EDGE, LANES), bf16),
            pltpu.VMEM((CHUNKS, N, ROWS + 16, LANES), bf16),
            pltpu.VMEM((CHUNKS, N, ROWS + 16, LANES), bf16),
            pltpu.VMEM((CHUNKS - 1, 64 * OWN, LANES), bf16),
            pltpu.VMEM((CHUNKS, N, HOME + 16, LANES), bf16),
            pltpu.VMEM((CHUNKS, 4, LANES, LANES), bf16),
            pltpu.VMEM((512, 512), bf16),
            pltpu.VMEM((N, HOME + 16, LANES), bf16),
            pltpu.VMEM((N, OWN, LANES), f32),
            pltpu.VMEM((N, OWN, LANES), f32),
            pltpu.VMEM((EDGE + EXT, LANES), f32),
            pltpu.VMEM((EDGE + EXT, LANES), f32),
            pltpu.VMEM((EXT, LANES), f32),
            pltpu.VMEM((EXT, LANES), f32),
            pltpu.VMEM((EXT, LANES), bf16),
            pltpu.VMEM((EXT, LANES), f32),
            pltpu.VMEM((EXT, LANES), f32),
            pltpu.VMEM((33, OWN, LANES), f32),
            pltpu.VMEM((2, 32, OWN, LANES), f32),
            pltpu.VMEM((2, 2, 128, LANES), f32),
            pltpu.VMEM((16, 2, 2, 112, LANES), bf16),
            pltpu.VMEM((2, 2, 64, 3 * LANES), f32),
            pltpu.VMEM((65, OWN, LANES), f32),
            dma((6,)),
            dma((6,)),
            dma((2 * CHUNKS, N)),
            dma((2 * CHUNKS, N)),
            dma((2 * CHUNKS,)),
            dma((8,)),
            dma((3,)),
        ],
        compiler_params=pltpu.CompilerParams(
            collective_id=0, has_side_effects=True, vmem_limit_bytes=56 * 2**20
        ),
        cost_estimate=pl.CostEstimate(
            flops=2 * 4 * 10**9, bytes_accessed=3 * 10**6, transcendentals=0
        ),
    )(pf, ps, og, up, fr, c1, c2, sk.reshape(1, LANES))


def solution(mesh):
    tok = P("seq", "ch")
    return jax.shard_map(
        body,
        mesh=mesh,
        in_specs=(tok,) * 5 + (P(None, "ch"), P(None, "ch"), P("ch")),
        out_specs=(tok,) * 3,
        check_vma=False,
    )
```

```python
from functools import partial

import jax
import jax.numpy as jnp
from jax import lax
from jax.experimental import pallas as pl
from jax.experimental.pallas import tpu as pltpu
from jax.sharding import PartitionSpec as P

f32 = jnp.float32
bf16 = jnp.bfloat16
MESH = pl.DeviceIdType.MESH
N = 16
LANES = 128
TOK = 1024
EXT = TOK + 16
OWN = 8
CHUNKS = 4
ROWS = 48
HOME = 32
EDGE = 16


PARTNERS = sorted(
    ((x, z, c) for x in range(2) for z in range(4) for c in range(2) if x + z + c),
    key=lambda k: -2 * k[0] - min(k[1], 4 - k[1]),
)


def partner(me, k):
    x = lax.rem(me // 8 + k[0], 2)
    z = lax.rem(lax.rem(me // 2, 4) + k[1], 4)
    return 8 * x + 2 * z + lax.rem(lax.rem(me, 2) + k[2], 2)


def kernel(
    pf_in, ps_in, og_in, up_in, fr_in, c1_in, c2_in, sk_in,
    out_first, out_second, out_filter,
    v_first, v_second, v_filter,
    pf, ps, og, up, fr, c1, c2, sk,
    halo, sbuf, rbuf, ybuf, rret, tok, pick, ylast, first, heads,
    pfx, psx, fc, sc, gg, fg, sg,
    gin, fin, frps, lss, accs, y,
    halo_send, halo_recv, send_sem, recv_sem, local_sem, in_sem, out_sem,
):
    me = lax.axis_index("seq")
    nxt = lax.rem(me + 1, N)
    prv = lax.rem(me + N - 1, N)

    barrier = pltpu.get_barrier_semaphore()

    def greet(k, _):
        pl.semaphore_signal(
            barrier, inc=1, device_id={"seq": lax.rem(me + k, N)}, device_id_type=MESH
        )
        return 0

    lax.fori_loop(1, N, greet, 0)

    fetched = [
        pltpu.make_async_copy(src, dst, in_sem.at[n])
        for n, (src, dst) in enumerate(
            (
                (og_in, og),
                (up_in, up),
                (fr_in, fr),
                (pf_in, pf),
                (ps_in, ps),
                (c1_in, c1),
                (c2_in, c2),
                (sk_in, sk),
            )
        )
    ]
    for copy in fetched:
        copy.start()

    row2 = lax.broadcasted_iota(jnp.int32, (512, 512), 0)
    col2 = lax.broadcasted_iota(jnp.int32, (512, 512), 1)
    picked = ((row2 & 6) << 6) + (row2 & 120) + ((row2 >> 7) << 1) + (row2 & 1)
    pick[...] = (picked == col2).astype(f32).astype(bf16)
    row1 = lax.broadcasted_iota(jnp.int32, (256, 256), 0)
    col1 = lax.broadcasted_iota(jnp.int32, (256, 256), 1)
    source = ((row1 & 64) << 1) + ((row1 >> 7) << 6) + 63 - (row1 & 63)
    flip = (source == col1).astype(f32).astype(bf16)
    eye = (row1 == col1)[0:LANES, 0:LANES].astype(f32).astype(bf16)

    def put(base, pairs):
        wide = [jnp.concatenate(pairs[n : n + 2], axis=1) for n in (0, 2)]
        turned = lax.dot_general(
            pick[...],
            jnp.concatenate(wide, axis=0),
            (((1,), (1,)), ((), ())),
            preferred_element_type=f32,
        )
        both = jnp.concatenate(
            [
                turned[:, LANES * n : LANES * (n + 1)].reshape(CHUNKS, N, OWN, LANES)
                for n in range(2)
            ],
            axis=2,
        ).astype(bf16)
        for chunk in range(CHUNKS):
            sbuf[chunk, :, base : base + 16, :] = both[chunk]

    def backwards(quarters):
        wide = jnp.concatenate(quarters[::-1], axis=1)
        back = jnp.dot(flip, wide, preferred_element_type=f32).astype(bf16)
        return [
            jnp.concatenate(
                [
                    back[LANES * z : LANES * (z + 1), LANES * q : LANES * (q + 1)]
                    for z in range(2)
                ],
                axis=1,
            )
            for q in range(len(quarters))
        ]

    def paired(blocks):
        return [jnp.concatenate(blocks[n : n + 2], axis=1) for n in range(0, len(blocks), 2)]

    def blocks_of(ref, size):
        return [ref[size * i : size * (i + 1), :] for i in range(TOK // size)]

    partners = [partner(me, k) for k in PARTNERS]

    def sent(chunk, to, frm):
        part = pl.ds(0, ROWS + 16 if isinstance(chunk, int) and chunk == 0 else ROWS)
        return sbuf.at[chunk, to, part], rbuf.at[chunk, frm, part]

    def exchange(chunk):
        for to in partners:
            src, dst = sent(chunk, to, me)
            pltpu.make_async_remote_copy(
                src_ref=src,
                dst_ref=dst,
                send_sem=send_sem.at[chunk, to],
                recv_sem=recv_sem.at[chunk, me],
                device_id={"seq": to},
                device_id_type=MESH,
            ).start()
        src, dst = sent(chunk, me, me)
        pltpu.make_async_copy(src, dst, local_sem.at[chunk]).start()

    def arrived(chunk):
        def go(k, _):
            frm = lax.rem(me + k, N)
            src, dst = sent(chunk, frm, frm)
            pltpu.make_async_remote_copy(
                src_ref=src,
                dst_ref=dst,
                send_sem=send_sem.at[chunk, frm],
                recv_sem=recv_sem.at[chunk, frm],
                device_id={"seq": frm},
                device_id_type=MESH,
            ).wait()
            return 0

        src, dst = sent(chunk, me, me)
        pltpu.make_async_copy(src, dst, local_sem.at[chunk]).wait()
        lax.fori_loop(1, N, go, 0)

    fetched[0].wait()
    fetched[1].wait()
    gg[0:TOK, :] = (og[...].astype(f32) * up[...].astype(f32)).astype(bf16)
    put(0, paired(blocks_of(gg, LANES)))
    fetched[2].wait()
    put(16, backwards(blocks_of(fr, 256)))

    for copy in fetched[3:]:
        copy.wait()

    def convolve(start, size):
        for x, w, dst in ((pfx, c1, fc), (psx, c2, sc)):
            dst[start : start + size, :] = (
                w[0:1, :] * x[EDGE + start : EDGE + start + size, :]
                + w[1:2, :] * x[EDGE + start - 1 : EDGE + start - 1 + size, :]
                + w[2:3, :] * x[EDGE + start - 2 : EDGE + start - 2 + size, :]
            )

    def products(quarters):
        return [
            (fc[256 * q : 256 * (q + 1), :] * sc[256 * q : 256 * (q + 1), :]).astype(bf16)
            for q in quarters
        ]

    for x, src in ((pfx, pf), (psx, ps)):
        x[EDGE : EDGE + TOK, :] = src[...].astype(f32)
    for x in (pfx, psx):
        x[0:EDGE, :] = jnp.zeros((EDGE, LANES), f32)
    convolve(0, TOK)
    put(32, backwards(products(range(4))))
    row3 = lax.broadcasted_iota(jnp.int32, (LANES, 2 * EDGE), 0)
    col3 = lax.broadcasted_iota(jnp.int32, (LANES, 2 * EDGE), 1)
    head = (row3 + col3 == 63) & (col3 < 2)
    tail = (row3 - col3 == 127 - 31) & (col3 >= 30)
    edge_pick = (head | tail).astype(f32).astype(bf16)
    edges = jnp.concatenate(
        [
            jnp.dot(
                edge_pick,
                jnp.concatenate([x[0:EDGE, :], x[TOK - EDGE : TOK, :]], axis=0),
                preferred_element_type=f32,
            ).astype(bf16)
            for x in (pf, ps)
        ],
        axis=0,
    )
    turned = [
        lax.dot_general(
            eye,
            edges[LANES * z : LANES * (z + 1)],
            (((1,), (1,)), ((), ())),
            preferred_element_type=f32,
        ).reshape(N, OWN, LANES)
        for z in range(2)
    ]
    sbuf[0, :, ROWS : ROWS + 16, :] = jnp.concatenate(turned, axis=1).astype(bf16)

    pl.semaphore_wait(barrier, N - 1)

    halos = [
        (pf_in, TOK - EDGE, nxt),
        (ps_in, TOK - EDGE, nxt),
        (pf_in, 0, prv),
        (ps_in, 0, prv),
        (og_in, 0, prv),
        (up_in, 0, prv),
    ]
    halo_copies = [
        pltpu.make_async_remote_copy(
            src_ref=ref.at[pl.ds(start, EDGE), :],
            dst_ref=halo.at[n],
            send_sem=halo_send.at[n],
            recv_sem=halo_recv.at[n],
            device_id={"seq": to},
            device_id_type=MESH,
        )
        for n, (ref, start, to) in enumerate(halos)
    ]
    for copy in halo_copies:
        copy.start()

    for chunk in range(CHUNKS):
        exchange(chunk)

    frps[...] = jnp.zeros_like(frps)
    gin[32] = jnp.zeros((OWN, LANES), f32)
    y[64] = jnp.zeros((OWN, LANES), f32)

    def unpack_gated(chunk):
        rows = rbuf[chunk, :, 0:16, :].astype(f32)
        gin[0:32, :, :] = rows.reshape(32, OWN, LANES)

    lane = lax.broadcasted_iota(jnp.int32, (OWN, LANES), 1)
    place = lax.broadcasted_iota(jnp.int32, (OWN, LANES), 0)

    def taps(ref):
        mine = lane == OWN * me + place
        for k in range(3):
            yield jnp.sum(jnp.where(mine, ref[k : k + 1, :], 0.0), axis=1, keepdims=True)

    def unpack_edges():
        weights = [list(taps(ref)) for ref in (c1, c2)]
        at63 = lane == 63
        last = [jnp.zeros((OWN, LANES), f32)] * 2
        for s in range(N):
            rows = rbuf[0, s, ROWS : ROWS + 16, :].astype(f32)
            conv = []
            for z in range(2):
                own = rows[OWN * z : OWN * (z + 1)]
                w = weights[z]
                one = jnp.where(at63, last[z], pltpu.roll(own, LANES - 1, 1))
                two = jnp.where(
                    at63, pltpu.roll(last[z], 1, 1), pltpu.roll(last[z], LANES - 1, 1)
                )
                conv.append(w[0] * own + w[1] * one + w[2] * two)
                last[z] = pltpu.roll(own, 64, 1)
            first[N - 1 - s] = (conv[0] * conv[1]).astype(bf16).astype(f32)

    def unpack_filter(chunk, f):
        for s in range(N):
            rows = rbuf[chunk, N - 1 - s, 16 * f + 16 : 16 * f + 32, :].astype(f32)
            fin[f, 2 * s : 2 * s + 2, :, :] = rows.reshape(2, OWN, LANES)

    row = lax.broadcasted_iota(jnp.int32, (64, LANES), 0)
    col = lax.broadcasted_iota(jnp.int32, (64, LANES), 1)
    mask = col - row <= 64
    low = col < 64
    fill = ((col == 62) | (col == 63))[0:N]

    def rolled(jj, ch):
        line = gin[jj // 4, pl.ds(2 * (jj % 4) + ch, 1), :]
        return pltpu.roll(
            jnp.broadcast_to(line, (64, LANES)), 65, 1, stride=1, stride_axis=0
        )

    def channel(ch, chunk):
        frp, ls, acc = frps.at[ch], lss.at[ch], accs.at[ch]
        for z in range(2):
            for f in range(2):
                for u in range(2):
                    frp[z, f, pl.ds(u, 32, stride=2), :] = fin[f, :, 4 * u + 2 * z + ch, :]
        at = pl.ds(3, N, stride=4)
        frp[0, 1, at, :] = jnp.where(
            fill, first[:, 2 * chunk + ch, :], frp[0, 1, at, :]
        )
        for r in range(16):
            for z in range(2):
                for f in range(2):
                    ls[r, z, f] = frp[z, f, pl.ds(r, 112), :].astype(bf16)
        acc[...] = jnp.zeros_like(acc)
        lines = [rolled(0, ch)]
        hankel = []

        def more_blocks(count):
            while len(hankel) < count:
                lines.append(rolled(min(len(lines), 128), ch))
                hankel.append(jnp.where(mask, lines[-2], lines[-1]).astype(bf16))

        for group in range(4):
            rows = 16 * (group + 1)
            top = 16 * (3 - group)
            left, right = [], []
            for k in range(16):
                j = 16 * group + k
                left.append(ls[15 - k, :, :, top : top + rows, :].reshape(4 * rows, LANES))
                more_blocks(2 * j + 4)
                for n in (2 * j, 2 * j + 1):
                    right.append(jnp.concatenate(hankel[n : n + 3], axis=1))
            left = jnp.concatenate(left, axis=1)
            right = jnp.concatenate(right, axis=0)
            both = jnp.dot(left, right[:, 0:256], preferred_element_type=f32)
            more = jnp.dot(left[2 * rows :], right[:, 256:], preferred_element_type=f32)
            acc[:, :, 0:rows, 0:256] += both.reshape(2, 2, rows, 256)
            acc[1, :, 0:rows, 256:] += more.reshape(2, rows, LANES)
        for f in range(2):
            moved = [
                pltpu.roll(acc[1, f, :, LANES * n : LANES * (n + 1)], 64, 1)
                for n in range(3)
            ]
            for h in range(2):
                total = acc[0, f, :, LANES * h : LANES * (h + 1)] + jnp.where(
                    low, moved[h], moved[h + 1]
                )
                y[0:64, 4 * h + 2 * f + ch, :] = total * (1.0, (TOK * N) ** -0.5)[f]
        heads[:, 2 * chunk + ch, :] = y[pl.ds(4, N, stride=4), ch, :]

    def home(chunk, to, frm):
        if isinstance(chunk, int) and chunk == CHUNKS - 1:
            return ylast.at[to], rret.at[chunk, frm]
        rows = pl.ds(pl.multiple_of(HOME * to, HOME), HOME)
        return ybuf.at[chunk, rows, :], rret.at[chunk, frm, pl.ds(0, HOME)]

    def back(chunk):
        for to in partners:
            src, dst = home(chunk, to, me)
            pltpu.make_async_remote_copy(
                src_ref=src,
                dst_ref=dst,
                send_sem=send_sem.at[CHUNKS + chunk, to],
                recv_sem=recv_sem.at[CHUNKS + chunk, me],
                device_id={"seq": to},
                device_id_type=MESH,
            ).start()
        src, dst = home(chunk, me, me)
        pltpu.make_async_copy(src, dst, local_sem.at[CHUNKS + chunk]).start()

    def back_done(chunk):
        def go(k, _):
            frm = lax.rem(me + k, N)
            src, dst = home(chunk, frm, frm)
            pltpu.make_async_remote_copy(
                src_ref=src,
                dst_ref=dst,
                send_sem=send_sem.at[CHUNKS + chunk, frm],
                recv_sem=recv_sem.at[CHUNKS + chunk, frm],
                device_id={"seq": frm},
                device_id_type=MESH,
            ).wait()
            return 0

        src, dst = home(chunk, me, me)
        pltpu.make_async_copy(src, dst, local_sem.at[CHUNKS + chunk]).wait()
        lax.fori_loop(1, N, go, 0)

    def one_chunk(chunk, _):
        @pl.when(chunk > 0)
        def _():
            arrived(chunk)

        unpack_gated(chunk)
        unpack_filter(chunk, 0)
        unpack_filter(chunk, 1)
        for ch in range(2):
            channel(ch, chunk)

        @pl.when(chunk < CHUNKS - 1)
        def _():
            ybuf[chunk] = y[0:64].reshape(64 * OWN, LANES).astype(bf16)
            back(chunk)

        return 0

    arrived(0)
    unpack_edges()
    lax.fori_loop(0, CHUNKS, one_chunk, 0)
    ylast[:, 0:HOME, :] = y[0:64].reshape(N, HOME, LANES).astype(bf16)
    ylast[:, HOME:, :] = jnp.concatenate([heads[...]] * 2, axis=1).astype(bf16)
    back(CHUNKS - 1)

    for copy in halo_copies:
        copy.wait()
    before = me > 0
    after = me < N - 1
    for n, x in enumerate((pfx, psx)):
        x[0:EDGE, :] = jnp.where(before, halo[n].astype(f32), 0.0)
        x[EDGE + TOK :, :] = halo[n + 2].astype(f32)
    convolve(0, EDGE)
    convolve(TOK, EXT - TOK)
    gg[TOK:, :] = jnp.where(after, halo[4].astype(f32) * halo[5].astype(f32), 0.0).astype(bf16)

    def columns(chunk, pair):
        both = rret[chunk, :, 16 * pair : 16 * pair + 16, :].astype(f32)
        both = both.reshape(N, 2, OWN, LANES)
        for n in range(2):
            turned = jnp.transpose(both[:, n].reshape(LANES, LANES))
            tok[chunk, 2 * pair + n] = turned.astype(bf16)

    skip = sk[...]

    def grads(start, size, mix):
        at = pl.ds(start, size)
        total = mix + skip * gg[at, :].astype(f32)
        fg[at, :] = (total * sc[at, :]).astype(bf16).astype(f32)
        sg[at, :] = (total * fc[at, :]).astype(bf16).astype(f32)

    for chunk in range(CHUNKS):
        back_done(chunk)
        for pair in range(2):
            columns(chunk, pair)
    following = rret[CHUNKS - 1, :, HOME:, :].astype(f32)[:, 0:OWN].reshape(LANES, LANES)
    grads(TOK, EXT - TOK, jnp.transpose(following)[0 : EXT - TOK])
    for i in range(4):
        both = jnp.dot(
            jnp.concatenate([tok[chunk, i] for chunk in range(CHUNKS)], axis=1),
            pick[...],
            preferred_element_type=f32,
        )
        for h in range(2):
            at = 256 * i + LANES * h
            grads(at, LANES, both[:, 256 * h : 256 * h + LANES])
            v_filter[at : at + LANES, :] = both[:, 256 * h + LANES : 256 * h + 256]
    copies = [
        pltpu.make_async_copy(src, dst, out_sem.at[n])
        for n, (src, dst) in enumerate(
            ((v_filter, out_filter), (v_first, out_first), (v_second, out_second))
        )
    ]
    copies[0].start()
    for x, w, dst, copy in ((fg, c1, v_first, copies[1]), (sg, c2, v_second, copies[2])):
        dst[...] = (
            w[0:1, :] * x[0:TOK, :]
            + w[1:2, :] * x[1 : TOK + 1, :]
            + w[2:3, :] * x[2 : TOK + 2, :]
        ).astype(bf16)
        copy.start()
    for copy in copies:
        copy.wait()


def body(pf, ps, og, up, fr, c1, c2, sk):
    hbm = pl.BlockSpec(memory_space=pltpu.HBM)
    dma = pltpu.SemaphoreType.DMA
    return pl.pallas_call(
        kernel,
        out_shape=(
            jax.ShapeDtypeStruct((TOK, LANES), bf16),
            jax.ShapeDtypeStruct((TOK, LANES), bf16),
            jax.ShapeDtypeStruct((TOK, LANES), f32),
        ),
        in_specs=[hbm] * 8,
        out_specs=(hbm,) * 3,
        scratch_shapes=[
            *[pltpu.VMEM((TOK, LANES), bf16)] * 2,
            pltpu.VMEM((TOK, LANES), f32),
            *[pltpu.VMEM((TOK, LANES), bf16)] * 5,
            *[pltpu.VMEM((3, LANES), f32)] * 2,
            pltpu.VMEM((1, LANES), f32),
            pltpu.VMEM((6, EDGE, LANES), bf16),
            pltpu.VMEM((CHUNKS, N, ROWS + 16, LANES), bf16),
            pltpu.VMEM((CHUNKS, N, ROWS + 16, LANES), bf16),
            pltpu.VMEM((CHUNKS - 1, 64 * OWN, LANES), bf16),
            pltpu.VMEM((CHUNKS, N, HOME + 16, LANES), bf16),
            pltpu.VMEM((CHUNKS, 4, LANES, LANES), bf16),
            pltpu.VMEM((512, 512), bf16),
            pltpu.VMEM((N, HOME + 16, LANES), bf16),
            pltpu.VMEM((N, OWN, LANES), f32),
            pltpu.VMEM((N, OWN, LANES), f32),
            pltpu.VMEM((EDGE + EXT, LANES), f32),
            pltpu.VMEM((EDGE + EXT, LANES), f32),
            pltpu.VMEM((EXT, LANES), f32),
            pltpu.VMEM((EXT, LANES), f32),
            pltpu.VMEM((EXT, LANES), bf16),
            pltpu.VMEM((EXT, LANES), f32),
            pltpu.VMEM((EXT, LANES), f32),
            pltpu.VMEM((33, OWN, LANES), f32),
            pltpu.VMEM((2, 32, OWN, LANES), f32),
            pltpu.VMEM((2, 2, 2, 128, LANES), f32),
            pltpu.VMEM((2, 16, 2, 2, 112, LANES), bf16),
            pltpu.VMEM((2, 2, 2, 64, 3 * LANES), f32),
            pltpu.VMEM((65, OWN, LANES), f32),
            dma((6,)),
            dma((6,)),
            dma((2 * CHUNKS, N)),
            dma((2 * CHUNKS, N)),
            dma((2 * CHUNKS,)),
            dma((8,)),
            dma((3,)),
        ],
        compiler_params=pltpu.CompilerParams(
            collective_id=0, has_side_effects=True, vmem_limit_bytes=56 * 2**20
        ),
        cost_estimate=pl.CostEstimate(
            flops=2 * 4 * 10**9, bytes_accessed=3 * 10**6, transcendentals=0
        ),
    )(pf, ps, og, up, fr, c1, c2, sk.reshape(1, LANES))


def solution(mesh):
    tok = P("seq", "ch")
    return jax.shard_map(
        body,
        mesh=mesh,
        in_specs=(tok,) * 5 + (P(None, "ch"), P(None, "ch"), P("ch")),
        out_specs=(tok,) * 3,
        check_vma=False,
    )
```

```python
from functools import partial

import jax
import jax.numpy as jnp
from jax import lax
from jax.experimental import pallas as pl
from jax.experimental.pallas import tpu as pltpu
from jax.sharding import PartitionSpec as P

f32 = jnp.float32
bf16 = jnp.bfloat16
MESH = pl.DeviceIdType.MESH
N = 16
LANES = 128
TOK = 1024
EXT = TOK + 16
OWN = 8
CHUNKS = 4
ROWS = 48
HOME = 32
EDGE = 16


PARTNERS = sorted(
    ((x, z, c) for x in range(2) for z in range(4) for c in range(2) if x + z + c),
    key=lambda k: -2 * k[0] - min(k[1], 4 - k[1]),
)


def partner(me, k):
    x = lax.rem(me // 8 + k[0], 2)
    z = lax.rem(lax.rem(me // 2, 4) + k[1], 4)
    return 8 * x + 2 * z + lax.rem(lax.rem(me, 2) + k[2], 2)


def kernel(
    pf_in, ps_in, og_in, up_in, fr_in, c1_in, c2_in, sk_in,
    out_first, out_second, out_filter,
    v_first, v_second, v_filter,
    pf, ps, og, up, fr, c1, c2, sk,
    halo, sbuf, rbuf, ybuf, rret, tok, pick, ylast, first, heads,
    pfx, psx, fc, sc, gg, fg, sg,
    gin, fin, frps, lss, accs, y,
    halo_send, halo_recv, send_sem, recv_sem, local_sem, in_sem, out_sem,
):
    me = lax.axis_index("seq")
    nxt = lax.rem(me + 1, N)
    prv = lax.rem(me + N - 1, N)

    barrier = pltpu.get_barrier_semaphore()

    def greet(k, _):
        pl.semaphore_signal(
            barrier, inc=1, device_id={"seq": lax.rem(me + k, N)}, device_id_type=MESH
        )
        return 0

    lax.fori_loop(1, N, greet, 0)

    fetched = [
        pltpu.make_async_copy(src, dst, in_sem.at[n])
        for n, (src, dst) in enumerate(
            (
                (og_in, og),
                (up_in, up),
                (fr_in, fr),
                (pf_in, pf),
                (ps_in, ps),
                (c1_in, c1),
                (c2_in, c2),
                (sk_in, sk),
            )
        )
    ]
    for copy in fetched:
        copy.start()

    row2 = lax.broadcasted_iota(jnp.int32, (512, 512), 0)
    col2 = lax.broadcasted_iota(jnp.int32, (512, 512), 1)
    picked = ((row2 & 6) << 6) + (row2 & 120) + ((row2 >> 7) << 1) + (row2 & 1)
    pick[...] = (picked == col2).astype(f32).astype(bf16)
    row1 = lax.broadcasted_iota(jnp.int32, (256, 256), 0)
    col1 = lax.broadcasted_iota(jnp.int32, (256, 256), 1)
    source = ((row1 & 64) << 1) + ((row1 >> 7) << 6) + 63 - (row1 & 63)
    flip = (source == col1).astype(f32).astype(bf16)
    eye = (row1 == col1)[0:LANES, 0:LANES].astype(f32).astype(bf16)

    def put(base, pairs):
        wide = [jnp.concatenate(pairs[n : n + 2], axis=1) for n in (0, 2)]
        turned = lax.dot_general(
            pick[...],
            jnp.concatenate(wide, axis=0),
            (((1,), (1,)), ((), ())),
            preferred_element_type=f32,
        )
        both = jnp.concatenate(
            [
                turned[:, LANES * n : LANES * (n + 1)].reshape(CHUNKS, N, OWN, LANES)
                for n in range(2)
            ],
            axis=2,
        ).astype(bf16)
        for chunk in range(CHUNKS):
            sbuf[chunk, :, base : base + 16, :] = both[chunk]

    def backwards(quarters):
        wide = jnp.concatenate(quarters[::-1], axis=1)
        back = jnp.dot(flip, wide, preferred_element_type=f32).astype(bf16)
        return [
            jnp.concatenate(
                [
                    back[LANES * z : LANES * (z + 1), LANES * q : LANES * (q + 1)]
                    for z in range(2)
                ],
                axis=1,
            )
            for q in range(len(quarters))
        ]

    def paired(blocks):
        return [jnp.concatenate(blocks[n : n + 2], axis=1) for n in range(0, len(blocks), 2)]

    def blocks_of(ref, size):
        return [ref[size * i : size * (i + 1), :] for i in range(TOK // size)]

    partners = [partner(me, k) for k in PARTNERS]

    def sent(chunk, to, frm):
        part = pl.ds(0, ROWS + 16 if isinstance(chunk, int) and chunk == 0 else ROWS)
        return sbuf.at[chunk, to, part], rbuf.at[chunk, frm, part]

    def exchange(chunk):
        for to in partners:
            src, dst = sent(chunk, to, me)
            pltpu.make_async_remote_copy(
                src_ref=src,
                dst_ref=dst,
                send_sem=send_sem.at[chunk, to],
                recv_sem=recv_sem.at[chunk, me],
                device_id={"seq": to},
                device_id_type=MESH,
            ).start()
        src, dst = sent(chunk, me, me)
        pltpu.make_async_copy(src, dst, local_sem.at[chunk]).start()

    def expected(chunk, frm):
        src, dst = sent(chunk, frm, frm)
        return pltpu.make_async_remote_copy(
            src_ref=src,
            dst_ref=dst,
            send_sem=send_sem.at[chunk, frm],
            recv_sem=recv_sem.at[chunk, frm],
            device_id={"seq": frm},
            device_id_type=MESH,
        )

    def all_sent(copy, chunk):
        def go(k, _):
            copy(chunk, lax.rem(me + k, N)).wait_send()
            return 0

        lax.fori_loop(1, N, go, 0)

    def arrived(chunk):
        def go(k, _):
            expected(chunk, lax.rem(me + k, N)).wait_recv()
            return 0

        src, dst = sent(chunk, me, me)
        pltpu.make_async_copy(src, dst, local_sem.at[chunk]).wait()
        lax.fori_loop(1, N, go, 0)

    fetched[0].wait()
    fetched[1].wait()
    gg[0:TOK, :] = (og[...].astype(f32) * up[...].astype(f32)).astype(bf16)
    put(0, paired(blocks_of(gg, LANES)))
    fetched[2].wait()
    put(16, backwards(blocks_of(fr, 256)))

    for copy in fetched[3:]:
        copy.wait()

    def convolve(start, size):
        for x, w, dst in ((pfx, c1, fc), (psx, c2, sc)):
            dst[start : start + size, :] = (
                w[0:1, :] * x[EDGE + start : EDGE + start + size, :]
                + w[1:2, :] * x[EDGE + start - 1 : EDGE + start - 1 + size, :]
                + w[2:3, :] * x[EDGE + start - 2 : EDGE + start - 2 + size, :]
            )

    def products(quarters):
        return [
            (fc[256 * q : 256 * (q + 1), :] * sc[256 * q : 256 * (q + 1), :]).astype(bf16)
            for q in quarters
        ]

    for x, src in ((pfx, pf), (psx, ps)):
        x[EDGE : EDGE + TOK, :] = src[...].astype(f32)
    for x in (pfx, psx):
        x[0:EDGE, :] = jnp.zeros((EDGE, LANES), f32)
    convolve(0, TOK)
    put(32, backwards(products(range(4))))
    row3 = lax.broadcasted_iota(jnp.int32, (LANES, 2 * EDGE), 0)
    col3 = lax.broadcasted_iota(jnp.int32, (LANES, 2 * EDGE), 1)
    head = (row3 + col3 == 63) & (col3 < 2)
    tail = (row3 - col3 == 127 - 31) & (col3 >= 30)
    edge_pick = (head | tail).astype(f32).astype(bf16)
    edges = jnp.concatenate(
        [
            jnp.dot(
                edge_pick,
                jnp.concatenate([x[0:EDGE, :], x[TOK - EDGE : TOK, :]], axis=0),
                preferred_element_type=f32,
            ).astype(bf16)
            for x in (pf, ps)
        ],
        axis=0,
    )
    turned = [
        lax.dot_general(
            eye,
            edges[LANES * z : LANES * (z + 1)],
            (((1,), (1,)), ((), ())),
            preferred_element_type=f32,
        ).reshape(N, OWN, LANES)
        for z in range(2)
    ]
    sbuf[0, :, ROWS : ROWS + 16, :] = jnp.concatenate(turned, axis=1).astype(bf16)

    pl.semaphore_wait(barrier, N - 1)

    halos = [
        (pf_in, TOK - EDGE, nxt),
        (ps_in, TOK - EDGE, nxt),
        (pf_in, 0, prv),
        (ps_in, 0, prv),
        (og_in, 0, prv),
        (up_in, 0, prv),
    ]
    halo_copies = [
        pltpu.make_async_remote_copy(
            src_ref=ref.at[pl.ds(start, EDGE), :],
            dst_ref=halo.at[n],
            send_sem=halo_send.at[n],
            recv_sem=halo_recv.at[n],
            device_id={"seq": to},
            device_id_type=MESH,
        )
        for n, (ref, start, to) in enumerate(halos)
    ]
    for copy in halo_copies:
        copy.start()

    for chunk in range(CHUNKS):
        exchange(chunk)

    frps[...] = jnp.zeros_like(frps)
    gin[32] = jnp.zeros((OWN, LANES), f32)
    y[64] = jnp.zeros((OWN, LANES), f32)

    def unpack_gated(chunk):
        rows = rbuf[chunk, :, 0:16, :].astype(f32)
        gin[0:32, :, :] = rows.reshape(32, OWN, LANES)

    lane = lax.broadcasted_iota(jnp.int32, (OWN, LANES), 1)
    place = lax.broadcasted_iota(jnp.int32, (OWN, LANES), 0)

    def taps(ref):
        mine = lane == OWN * me + place
        for k in range(3):
            yield jnp.sum(jnp.where(mine, ref[k : k + 1, :], 0.0), axis=1, keepdims=True)

    def unpack_edges():
        weights = [list(taps(ref)) for ref in (c1, c2)]
        at63 = lane == 63
        last = [jnp.zeros((OWN, LANES), f32)] * 2
        for s in range(N):
            rows = rbuf[0, s, ROWS : ROWS + 16, :].astype(f32)
            conv = []
            for z in range(2):
                own = rows[OWN * z : OWN * (z + 1)]
                w = weights[z]
                one = jnp.where(at63, last[z], pltpu.roll(own, LANES - 1, 1))
                two = jnp.where(
                    at63, pltpu.roll(last[z], 1, 1), pltpu.roll(last[z], LANES - 1, 1)
                )
                conv.append(w[0] * own + w[1] * one + w[2] * two)
                last[z] = pltpu.roll(own, 64, 1)
            first[N - 1 - s] = (conv[0] * conv[1]).astype(bf16).astype(f32)

    def unpack_filter(chunk, f):
        for s in range(N):
            rows = rbuf[chunk, N - 1 - s, 16 * f + 16 : 16 * f + 32, :].astype(f32)
            fin[f, 2 * s : 2 * s + 2, :, :] = rows.reshape(2, OWN, LANES)

    row = lax.broadcasted_iota(jnp.int32, (64, LANES), 0)
    col = lax.broadcasted_iota(jnp.int32, (64, LANES), 1)
    mask = col - row <= 64
    low = col < 64
    fill = ((col == 62) | (col == 63))[0:N]

    def rolled(jj, ch):
        line = gin[jj // 4, pl.ds(2 * (jj % 4) + ch, 1), :]
        return pltpu.roll(
            jnp.broadcast_to(line, (64, LANES)), 65, 1, stride=1, stride_axis=0
        )

    def channel(ch, chunk):
        frp, ls, acc = frps.at[ch], lss.at[ch], accs.at[ch]
        for z in range(2):
            for f in range(2):
                for u in range(2):
                    frp[z, f, pl.ds(u, 32, stride=2), :] = fin[f, :, 4 * u + 2 * z + ch, :]
        at = pl.ds(3, N, stride=4)
        frp[0, 1, at, :] = jnp.where(
            fill, first[:, 2 * chunk + ch, :], frp[0, 1, at, :]
        )
        for r in range(16):
            for z in range(2):
                for f in range(2):
                    ls[r, z, f] = frp[z, f, pl.ds(r, 112), :].astype(bf16)
        acc[...] = jnp.zeros_like(acc)
        lines = [rolled(0, ch)]
        hankel = []

        def more_blocks(count):
            while len(hankel) < count:
                lines.append(rolled(min(len(lines), 128), ch))
                hankel.append(jnp.where(mask, lines[-2], lines[-1]).astype(bf16))

        for group in range(4):
            rows = 16 * (group + 1)
            top = 16 * (3 - group)
            left, right = [], []
            for k in range(16):
                j = 16 * group + k
                left.append(ls[15 - k, :, :, top : top + rows, :].reshape(4 * rows, LANES))
                more_blocks(2 * j + 4)
                for n in (2 * j, 2 * j + 1):
                    right.append(jnp.concatenate(hankel[n : n + 3], axis=1))
            left = jnp.concatenate(left, axis=1)
            right = jnp.concatenate(right, axis=0)
            both = jnp.dot(left, right[:, 0:256], preferred_element_type=f32)
            more = jnp.dot(left[2 * rows :], right[:, 256:], preferred_element_type=f32)
            acc[:, :, 0:rows, 0:256] += both.reshape(2, 2, rows, 256)
            acc[1, :, 0:rows, 256:] += more.reshape(2, rows, LANES)
        for f in range(2):
            moved = [
                pltpu.roll(acc[1, f, :, LANES * n : LANES * (n + 1)], 64, 1)
                for n in range(3)
            ]
            for h in range(2):
                total = acc[0, f, :, LANES * h : LANES * (h + 1)] + jnp.where(
                    low, moved[h], moved[h + 1]
                )
                y[0:64, 4 * h + 2 * f + ch, :] = total * (1.0, (TOK * N) ** -0.5)[f]
        heads[:, 2 * chunk + ch, :] = y[pl.ds(4, N, stride=4), ch, :]

    def home(chunk, to, frm):
        if isinstance(chunk, int) and chunk == CHUNKS - 1:
            return ylast.at[to], rret.at[chunk, frm]
        rows = pl.ds(pl.multiple_of(HOME * to, HOME), HOME)
        return ybuf.at[chunk, rows, :], rret.at[chunk, frm, pl.ds(0, HOME)]

    def back(chunk):
        for to in partners:
            src, dst = home(chunk, to, me)
            pltpu.make_async_remote_copy(
                src_ref=src,
                dst_ref=dst,
                send_sem=send_sem.at[CHUNKS + chunk, to],
                recv_sem=recv_sem.at[CHUNKS + chunk, me],
                device_id={"seq": to},
                device_id_type=MESH,
            ).start()
        src, dst = home(chunk, me, me)
        pltpu.make_async_copy(src, dst, local_sem.at[CHUNKS + chunk]).start()

    def returned(chunk, frm):
        src, dst = home(chunk, frm, frm)
        return pltpu.make_async_remote_copy(
            src_ref=src,
            dst_ref=dst,
            send_sem=send_sem.at[CHUNKS + chunk, frm],
            recv_sem=recv_sem.at[CHUNKS + chunk, frm],
            device_id={"seq": frm},
            device_id_type=MESH,
        )

    def back_done(chunk):
        def go(k, _):
            returned(chunk, lax.rem(me + k, N)).wait_recv()
            return 0

        src, dst = home(chunk, me, me)
        pltpu.make_async_copy(src, dst, local_sem.at[CHUNKS + chunk]).wait()
        lax.fori_loop(1, N, go, 0)

    def one_chunk(chunk, _):
        @pl.when(chunk > 0)
        def _():
            arrived(chunk)

        unpack_gated(chunk)
        unpack_filter(chunk, 0)
        unpack_filter(chunk, 1)
        for ch in range(2):
            channel(ch, chunk)

        @pl.when(chunk < CHUNKS - 1)
        def _():
            ybuf[chunk] = y[0:64].reshape(64 * OWN, LANES).astype(bf16)
            back(chunk)

        return 0

    arrived(0)
    unpack_edges()
    lax.fori_loop(0, CHUNKS, one_chunk, 0)
    ylast[:, 0:HOME, :] = y[0:64].reshape(N, HOME, LANES).astype(bf16)
    ylast[:, HOME:, :] = jnp.concatenate([heads[...]] * 2, axis=1).astype(bf16)
    back(CHUNKS - 1)
    for chunk in range(CHUNKS):
        all_sent(expected, chunk)

    for copy in halo_copies:
        copy.wait()
    before = me > 0
    after = me < N - 1
    for n, x in enumerate((pfx, psx)):
        x[0:EDGE, :] = jnp.where(before, halo[n].astype(f32), 0.0)
        x[EDGE + TOK :, :] = halo[n + 2].astype(f32)
    convolve(0, EDGE)
    convolve(TOK, EXT - TOK)
    gg[TOK:, :] = jnp.where(after, halo[4].astype(f32) * halo[5].astype(f32), 0.0).astype(bf16)

    def columns(chunk, pair):
        both = rret[chunk, :, 16 * pair : 16 * pair + 16, :].astype(f32)
        both = both.reshape(N, 2, OWN, LANES)
        for n in range(2):
            turned = jnp.transpose(both[:, n].reshape(LANES, LANES))
            tok[chunk, 2 * pair + n] = turned.astype(bf16)

    skip = sk[...]

    def grads(start, size, mix):
        at = pl.ds(start, size)
        total = mix + skip * gg[at, :].astype(f32)
        fg[at, :] = (total * sc[at, :]).astype(bf16).astype(f32)
        sg[at, :] = (total * fc[at, :]).astype(bf16).astype(f32)

    for chunk in range(CHUNKS):
        back_done(chunk)
        for pair in range(2):
            columns(chunk, pair)
    following = rret[CHUNKS - 1, :, HOME:, :].astype(f32)[:, 0:OWN].reshape(LANES, LANES)
    grads(TOK, EXT - TOK, jnp.transpose(following)[0 : EXT - TOK])
    for i in range(4):
        both = jnp.dot(
            jnp.concatenate([tok[chunk, i] for chunk in range(CHUNKS)], axis=1),
            pick[...],
            preferred_element_type=f32,
        )
        for h in range(2):
            at = 256 * i + LANES * h
            grads(at, LANES, both[:, 256 * h : 256 * h + LANES])
            v_filter[at : at + LANES, :] = both[:, 256 * h + LANES : 256 * h + 256]
    copies = [
        pltpu.make_async_copy(src, dst, out_sem.at[n])
        for n, (src, dst) in enumerate(
            ((v_filter, out_filter), (v_first, out_first), (v_second, out_second))
        )
    ]
    copies[0].start()
    for x, w, dst, copy in ((fg, c1, v_first, copies[1]), (sg, c2, v_second, copies[2])):
        dst[...] = (
            w[0:1, :] * x[0:TOK, :]
            + w[1:2, :] * x[1 : TOK + 1, :]
            + w[2:3, :] * x[2 : TOK + 2, :]
        ).astype(bf16)
        copy.start()
    for chunk in range(CHUNKS):
        all_sent(returned, chunk)
    for copy in copies:
        copy.wait()


def body(pf, ps, og, up, fr, c1, c2, sk):
    hbm = pl.BlockSpec(memory_space=pltpu.HBM)
    dma = pltpu.SemaphoreType.DMA
    return pl.pallas_call(
        kernel,
        out_shape=(
            jax.ShapeDtypeStruct((TOK, LANES), bf16),
            jax.ShapeDtypeStruct((TOK, LANES), bf16),
            jax.ShapeDtypeStruct((TOK, LANES), f32),
        ),
        in_specs=[hbm] * 8,
        out_specs=(hbm,) * 3,
        scratch_shapes=[
            *[pltpu.VMEM((TOK, LANES), bf16)] * 2,
            pltpu.VMEM((TOK, LANES), f32),
            *[pltpu.VMEM((TOK, LANES), bf16)] * 5,
            *[pltpu.VMEM((3, LANES), f32)] * 2,
            pltpu.VMEM((1, LANES), f32),
            pltpu.VMEM((6, EDGE, LANES), bf16),
            pltpu.VMEM((CHUNKS, N, ROWS + 16, LANES), bf16),
            pltpu.VMEM((CHUNKS, N, ROWS + 16, LANES), bf16),
            pltpu.VMEM((CHUNKS - 1, 64 * OWN, LANES), bf16),
            pltpu.VMEM((CHUNKS, N, HOME + 16, LANES), bf16),
            pltpu.VMEM((CHUNKS, 4, LANES, LANES), bf16),
            pltpu.VMEM((512, 512), bf16),
            pltpu.VMEM((N, HOME + 16, LANES), bf16),
            pltpu.VMEM((N, OWN, LANES), f32),
            pltpu.VMEM((N, OWN, LANES), f32),
            pltpu.VMEM((EDGE + EXT, LANES), f32),
            pltpu.VMEM((EDGE + EXT, LANES), f32),
            pltpu.VMEM((EXT, LANES), f32),
            pltpu.VMEM((EXT, LANES), f32),
            pltpu.VMEM((EXT, LANES), bf16),
            pltpu.VMEM((EXT, LANES), f32),
            pltpu.VMEM((EXT, LANES), f32),
            pltpu.VMEM((33, OWN, LANES), f32),
            pltpu.VMEM((2, 32, OWN, LANES), f32),
            pltpu.VMEM((2, 2, 2, 128, LANES), f32),
            pltpu.VMEM((2, 16, 2, 2, 112, LANES), bf16),
            pltpu.VMEM((2, 2, 2, 64, 3 * LANES), f32),
            pltpu.VMEM((65, OWN, LANES), f32),
            dma((6,)),
            dma((6,)),
            dma((2 * CHUNKS, N)),
            dma((2 * CHUNKS, N)),
            dma((2 * CHUNKS,)),
            dma((8,)),
            dma((3,)),
        ],
        compiler_params=pltpu.CompilerParams(
            collective_id=0, has_side_effects=True, vmem_limit_bytes=56 * 2**20
        ),
        cost_estimate=pl.CostEstimate(
            flops=2 * 4 * 10**9, bytes_accessed=3 * 10**6, transcendentals=0
        ),
    )(pf, ps, og, up, fr, c1, c2, sk.reshape(1, LANES))


def solution(mesh):
    tok = P("seq", "ch")
    return jax.shard_map(
        body,
        mesh=mesh,
        in_specs=(tok,) * 5 + (P(None, "ch"), P(None, "ch"), P("ch")),
        out_specs=(tok,) * 3,
        check_vma=False,
    )
```

```python
from functools import partial

import jax
import jax.numpy as jnp
from jax import lax
from jax.experimental import pallas as pl
from jax.experimental.pallas import tpu as pltpu
from jax.sharding import PartitionSpec as P

f32 = jnp.float32
bf16 = jnp.bfloat16
MESH = pl.DeviceIdType.MESH
N = 16
LANES = 128
TOK = 1024
EXT = TOK + 16
OWN = 8
CHUNKS = 4
ROWS = 48
HOME = 32
EDGE = 16


PARTNERS = sorted(
    ((x, z, c) for x in range(2) for z in range(4) for c in range(2) if x + z + c),
    key=lambda k: -2 * k[0] - min(k[1], 4 - k[1]),
)


def partner(me, k):
    x = lax.rem(me // 8 + k[0], 2)
    z = lax.rem(lax.rem(me // 2, 4) + k[1], 4)
    return 8 * x + 2 * z + lax.rem(lax.rem(me, 2) + k[2], 2)


def kernel(
    pf_in, ps_in, og_in, up_in, fr_in, c1_in, c2_in, sk_in,
    out_first, out_second, out_filter,
    v_first, v_second, v_filter,
    pf, ps, og, up, fr, c1, c2, sk,
    halo, sbuf, rbuf, ybuf, rret, tok, pick, ylast, first, heads,
    pfx, psx, fc, sc, gg, fg, sg,
    gin, fin, frps, lss, accs, y,
    halo_send, halo_recv, send_sem, recv_sem, local_sem, in_sem, out_sem,
):
    me = lax.axis_index("seq")
    nxt = lax.rem(me + 1, N)
    prv = lax.rem(me + N - 1, N)

    barrier = pltpu.get_barrier_semaphore()

    def greet(k, _):
        pl.semaphore_signal(
            barrier, inc=1, device_id={"seq": lax.rem(me + k, N)}, device_id_type=MESH
        )
        return 0

    lax.fori_loop(1, N, greet, 0)

    fetched = [
        pltpu.make_async_copy(src, dst, in_sem.at[n])
        for n, (src, dst) in enumerate(
            (
                (og_in, og),
                (up_in, up),
                (fr_in, fr),
                (pf_in, pf),
                (ps_in, ps),
                (c1_in, c1),
                (c2_in, c2),
                (sk_in, sk),
            )
        )
    ]
    for copy in fetched:
        copy.start()

    row2 = lax.broadcasted_iota(jnp.int32, (512, 512), 0)
    col2 = lax.broadcasted_iota(jnp.int32, (512, 512), 1)
    picked = ((row2 & 6) << 6) + (row2 & 120) + ((row2 >> 7) << 1) + (row2 & 1)
    pick[...] = (picked == col2).astype(f32).astype(bf16)
    row1 = lax.broadcasted_iota(jnp.int32, (256, 256), 0)
    col1 = lax.broadcasted_iota(jnp.int32, (256, 256), 1)
    source = ((row1 & 64) << 1) + ((row1 >> 7) << 6) + 63 - (row1 & 63)
    flip = (source == col1).astype(f32).astype(bf16)
    eye = (row1 == col1)[0:LANES, 0:LANES].astype(f32).astype(bf16)

    def put(base, pairs):
        wide = [jnp.concatenate(pairs[n : n + 2], axis=1) for n in (0, 2)]
        turned = lax.dot_general(
            pick[...],
            jnp.concatenate(wide, axis=0),
            (((1,), (1,)), ((), ())),
            preferred_element_type=f32,
        )
        both = jnp.concatenate(
            [
                turned[:, LANES * n : LANES * (n + 1)].reshape(CHUNKS, N, OWN, LANES)
                for n in range(2)
            ],
            axis=2,
        ).astype(bf16)
        for chunk in range(CHUNKS):
            sbuf[chunk, :, base : base + 16, :] = both[chunk]

    def backwards(quarters):
        wide = jnp.concatenate(quarters[::-1], axis=1)
        back = jnp.dot(flip, wide, preferred_element_type=f32).astype(bf16)
        return [
            jnp.concatenate(
                [
                    back[LANES * z : LANES * (z + 1), LANES * q : LANES * (q + 1)]
                    for z in range(2)
                ],
                axis=1,
            )
            for q in range(len(quarters))
        ]

    def paired(blocks):
        return [jnp.concatenate(blocks[n : n + 2], axis=1) for n in range(0, len(blocks), 2)]

    def blocks_of(ref, size):
        return [ref[size * i : size * (i + 1), :] for i in range(TOK // size)]

    partners = [partner(me, k) for k in PARTNERS]

    def sent(chunk, to, frm):
        part = pl.ds(0, ROWS + 16 if isinstance(chunk, int) and chunk == 0 else ROWS)
        return sbuf.at[chunk, to, part], rbuf.at[chunk, frm, part]

    def exchange(chunk):
        for to in partners:
            src, dst = sent(chunk, to, me)
            pltpu.make_async_remote_copy(
                src_ref=src,
                dst_ref=dst,
                send_sem=send_sem.at[chunk, to],
                recv_sem=recv_sem.at[chunk, me],
                device_id={"seq": to},
                device_id_type=MESH,
            ).start()
        src, dst = sent(chunk, me, me)
        pltpu.make_async_copy(src, dst, local_sem.at[chunk]).start()

    def expected(chunk, frm):
        src, dst = sent(chunk, frm, frm)
        return pltpu.make_async_remote_copy(
            src_ref=src,
            dst_ref=dst,
            send_sem=send_sem.at[chunk, frm],
            recv_sem=recv_sem.at[chunk, frm],
            device_id={"seq": frm},
            device_id_type=MESH,
        )

    def all_sent(copy, chunk):
        def go(k, _):
            copy(chunk, lax.rem(me + k, N)).wait_send()
            return 0

        lax.fori_loop(1, N, go, 0)

    def arrived(chunk):
        def go(k, _):
            expected(chunk, lax.rem(me + k, N)).wait_recv()
            return 0

        src, dst = sent(chunk, me, me)
        pltpu.make_async_copy(src, dst, local_sem.at[chunk]).wait()
        lax.fori_loop(1, N, go, 0)

    fetched[0].wait()
    fetched[1].wait()
    gg[0:TOK, :] = (og[...].astype(f32) * up[...].astype(f32)).astype(bf16)
    put(0, paired(blocks_of(gg, LANES)))
    fetched[2].wait()
    put(16, backwards(blocks_of(fr, 256)))

    for copy in fetched[3:]:
        copy.wait()

    def convolve(start, size):
        for x, w, dst in ((pfx, c1, fc), (psx, c2, sc)):
            dst[start : start + size, :] = (
                w[0:1, :] * x[EDGE + start : EDGE + start + size, :]
                + w[1:2, :] * x[EDGE + start - 1 : EDGE + start - 1 + size, :]
                + w[2:3, :] * x[EDGE + start - 2 : EDGE + start - 2 + size, :]
            )

    def products(quarters):
        return [
            (fc[256 * q : 256 * (q + 1), :] * sc[256 * q : 256 * (q + 1), :]).astype(bf16)
            for q in quarters
        ]

    for x, src in ((pfx, pf), (psx, ps)):
        x[EDGE : EDGE + TOK, :] = src[...].astype(f32)
    for x in (pfx, psx):
        x[0:EDGE, :] = jnp.zeros((EDGE, LANES), f32)
    convolve(0, TOK)
    put(32, backwards(products(range(4))))
    row3 = lax.broadcasted_iota(jnp.int32, (LANES, 2 * EDGE), 0)
    col3 = lax.broadcasted_iota(jnp.int32, (LANES, 2 * EDGE), 1)
    head = (row3 + col3 == 63) & (col3 < 2)
    tail = (row3 - col3 == 127 - 31) & (col3 >= 30)
    edge_pick = (head | tail).astype(f32).astype(bf16)
    edges = jnp.concatenate(
        [
            jnp.dot(
                edge_pick,
                jnp.concatenate([x[0:EDGE, :], x[TOK - EDGE : TOK, :]], axis=0),
                preferred_element_type=f32,
            ).astype(bf16)
            for x in (pf, ps)
        ],
        axis=0,
    )
    turned = [
        lax.dot_general(
            eye,
            edges[LANES * z : LANES * (z + 1)],
            (((1,), (1,)), ((), ())),
            preferred_element_type=f32,
        ).reshape(N, OWN, LANES)
        for z in range(2)
    ]
    sbuf[0, :, ROWS : ROWS + 16, :] = jnp.concatenate(turned, axis=1).astype(bf16)

    pl.semaphore_wait(barrier, N - 1)

    halos = [
        (pf_in, TOK - EDGE, nxt),
        (ps_in, TOK - EDGE, nxt),
        (pf_in, 0, prv),
        (ps_in, 0, prv),
        (og_in, 0, prv),
        (up_in, 0, prv),
    ]
    halo_copies = [
        pltpu.make_async_remote_copy(
            src_ref=ref.at[pl.ds(start, EDGE), :],
            dst_ref=halo.at[n],
            send_sem=halo_send.at[n],
            recv_sem=halo_recv.at[n],
            device_id={"seq": to},
            device_id_type=MESH,
        )
        for n, (ref, start, to) in enumerate(halos)
    ]
    for copy in halo_copies:
        copy.start()

    for chunk in range(CHUNKS):
        exchange(chunk)

    frps[...] = jnp.zeros_like(frps)
    gin[32] = jnp.zeros((OWN, LANES), f32)
    y[64] = jnp.zeros((OWN, LANES), f32)

    def unpack_gated(chunk):
        rows = rbuf[chunk, :, 0:16, :].astype(f32)
        gin[0:32, :, :] = rows.reshape(32, OWN, LANES)

    lane = lax.broadcasted_iota(jnp.int32, (OWN, LANES), 1)
    place = lax.broadcasted_iota(jnp.int32, (OWN, LANES), 0)

    def taps(ref):
        mine = lane == OWN * me + place
        for k in range(3):
            yield jnp.sum(jnp.where(mine, ref[k : k + 1, :], 0.0), axis=1, keepdims=True)

    def unpack_edges():
        weights = [list(taps(ref)) for ref in (c1, c2)]
        at63 = lane == 63
        last = [jnp.zeros((OWN, LANES), f32)] * 2
        for s in range(N):
            rows = rbuf[0, s, ROWS : ROWS + 16, :].astype(f32)
            conv = []
            for z in range(2):
                own = rows[OWN * z : OWN * (z + 1)]
                w = weights[z]
                one = jnp.where(at63, last[z], pltpu.roll(own, LANES - 1, 1))
                two = jnp.where(
                    at63, pltpu.roll(last[z], 1, 1), pltpu.roll(last[z], LANES - 1, 1)
                )
                conv.append(w[0] * own + w[1] * one + w[2] * two)
                last[z] = pltpu.roll(own, 64, 1)
            first[N - 1 - s] = (conv[0] * conv[1]).astype(bf16).astype(f32)

    def unpack_filter(chunk, f):
        for s in range(N):
            rows = rbuf[chunk, N - 1 - s, 16 * f + 16 : 16 * f + 32, :].astype(f32)
            fin[f, 2 * s : 2 * s + 2, :, :] = rows.reshape(2, OWN, LANES)

    row = lax.broadcasted_iota(jnp.int32, (64, LANES), 0)
    col = lax.broadcasted_iota(jnp.int32, (64, LANES), 1)
    mask = col - row <= 64
    low = col < 64
    fill = ((col == 62) | (col == 63))[0:N]

    def rolled(jj, ch):
        line = gin[jj // 4, pl.ds(2 * (jj % 4) + ch, 1), :]
        return pltpu.roll(
            jnp.broadcast_to(line, (64, LANES)), 65, 1, stride=1, stride_axis=0
        )

    def channel(ch, chunk):
        frp, ls, acc = frps.at[ch], lss.at[ch], accs.at[ch]
        for z in range(2):
            for f in range(2):
                for u in range(2):
                    frp[z, f, pl.ds(u, 32, stride=2), :] = fin[f, :, 4 * u + 2 * z + ch, :]
        at = pl.ds(3, N, stride=4)
        frp[0, 1, at, :] = jnp.where(
            fill, first[:, 2 * chunk + ch, :], frp[0, 1, at, :]
        )
        for r in range(16):
            for z in range(2):
                for f in range(2):
                    ls[r, z, f] = frp[z, f, pl.ds(r, 112), :].astype(bf16)
        acc[...] = jnp.zeros_like(acc)
        lines = [rolled(0, ch)]
        hankel = []

        def more_blocks(count):
            while len(hankel) < count:
                lines.append(rolled(min(len(lines), 128), ch))
                hankel.append(jnp.where(mask, lines[-2], lines[-1]).astype(bf16))

        for group in range(4):
            rows = 16 * (group + 1)
            top = 16 * (3 - group)
            left, right = [], []
            for k in range(16):
                j = 16 * group + k
                left.append(ls[15 - k, :, :, top : top + rows, :].reshape(4 * rows, LANES))
                more_blocks(2 * j + 4)
                for n in (2 * j, 2 * j + 1):
                    right.append(jnp.concatenate(hankel[n : n + 3], axis=1))
            left = jnp.concatenate(left, axis=1)
            right = jnp.concatenate(right, axis=0)
            both = jnp.dot(left, right[:, 0:256], preferred_element_type=f32)
            more = jnp.dot(left[2 * rows :], right[:, 256:], preferred_element_type=f32)
            acc[:, :, 0:rows, 0:256] += both.reshape(2, 2, rows, 256)
            acc[1, :, 0:rows, 256:] += more.reshape(2, rows, LANES)
        for f in range(2):
            moved = [
                pltpu.roll(acc[1, f, :, LANES * n : LANES * (n + 1)], 64, 1)
                for n in range(3)
            ]
            for h in range(2):
                total = acc[0, f, :, LANES * h : LANES * (h + 1)] + jnp.where(
                    low, moved[h], moved[h + 1]
                )
                y[0:64, 4 * h + 2 * f + ch, :] = total * (1.0, (TOK * N) ** -0.5)[f]
        heads[:, 2 * chunk + ch, :] = y[pl.ds(4, N, stride=4), ch, :]

    def home(chunk, to, frm):
        if isinstance(chunk, int) and chunk == CHUNKS - 1:
            return ylast.at[to], rret.at[chunk, frm]
        rows = pl.ds(pl.multiple_of(HOME * to, HOME), HOME)
        return ybuf.at[chunk, rows, :], rret.at[chunk, frm, pl.ds(0, HOME)]

    def back(chunk):
        for to in partners:
            src, dst = home(chunk, to, me)
            pltpu.make_async_remote_copy(
                src_ref=src,
                dst_ref=dst,
                send_sem=send_sem.at[CHUNKS + chunk, to],
                recv_sem=recv_sem.at[CHUNKS + chunk, me],
                device_id={"seq": to},
                device_id_type=MESH,
            ).start()
        src, dst = home(chunk, me, me)
        pltpu.make_async_copy(src, dst, local_sem.at[CHUNKS + chunk]).start()

    def returned(chunk, frm):
        src, dst = home(chunk, frm, frm)
        return pltpu.make_async_remote_copy(
            src_ref=src,
            dst_ref=dst,
            send_sem=send_sem.at[CHUNKS + chunk, frm],
            recv_sem=recv_sem.at[CHUNKS + chunk, frm],
            device_id={"seq": frm},
            device_id_type=MESH,
        )

    def back_done(chunk):
        def go(k, _):
            returned(chunk, lax.rem(me + k, N)).wait_recv()
            return 0

        src, dst = home(chunk, me, me)
        pltpu.make_async_copy(src, dst, local_sem.at[CHUNKS + chunk]).wait()
        lax.fori_loop(1, N, go, 0)

    def one_chunk(chunk, _):
        @pl.when(chunk > 0)
        def _():
            arrived(chunk)

        unpack_gated(chunk)
        unpack_filter(chunk, 0)
        unpack_filter(chunk, 1)
        for ch in range(2):
            channel(ch, chunk)

        @pl.when(chunk < CHUNKS - 1)
        def _():
            ybuf[chunk] = y[0:64].reshape(64 * OWN, LANES).astype(bf16)
            back(chunk)

        return 0

    arrived(0)
    unpack_edges()
    lax.fori_loop(0, CHUNKS, one_chunk, 0)
    ylast[:, 0:HOME, :] = y[0:64].reshape(N, HOME, LANES).astype(bf16)
    ylast[:, HOME:, :] = jnp.concatenate([heads[...]] * 2, axis=1).astype(bf16)
    back(CHUNKS - 1)
    for chunk in range(CHUNKS):
        all_sent(expected, chunk)

    for copy in halo_copies:
        copy.wait()
    before = me > 0
    after = me < N - 1
    for n, x in enumerate((pfx, psx)):
        x[0:EDGE, :] = jnp.where(before, halo[n].astype(f32), 0.0)
        x[EDGE + TOK :, :] = halo[n + 2].astype(f32)
    convolve(0, EDGE)
    convolve(TOK, EXT - TOK)
    gg[TOK:, :] = jnp.where(after, halo[4].astype(f32) * halo[5].astype(f32), 0.0).astype(bf16)

    def columns(chunk, pair):
        both = rret[chunk, :, 16 * pair : 16 * pair + 16, :].astype(f32)
        both = both.reshape(N, 2, OWN, LANES)
        for n in range(2):
            turned = jnp.transpose(both[:, n].reshape(LANES, LANES))
            tok[chunk, 2 * pair + n] = turned.astype(bf16)

    skip = sk[...]

    def grads(start, size, mix):
        at = pl.ds(start, size)
        total = mix + skip * gg[at, :].astype(f32)
        fg[at, :] = (total * sc[at, :]).astype(bf16).astype(f32)
        sg[at, :] = (total * fc[at, :]).astype(bf16).astype(f32)

    for chunk in range(CHUNKS):
        back_done(chunk)
        for pair in range(2):
            columns(chunk, pair)
    following = rret[CHUNKS - 1, :, HOME:, :].astype(f32)[:, 0:OWN].reshape(LANES, LANES)
    grads(TOK, EXT - TOK, jnp.transpose(following)[0 : EXT - TOK])
    for i in range(4):
        both = jnp.dot(
            jnp.concatenate([tok[chunk, i] for chunk in range(CHUNKS)], axis=1),
            pick[...],
            preferred_element_type=f32,
        )
        for h in range(2):
            at = 256 * i + LANES * h
            grads(at, LANES, both[:, 256 * h : 256 * h + LANES])
            v_filter[at : at + LANES, :] = both[:, 256 * h + LANES : 256 * h + 256]
    copies = [
        pltpu.make_async_copy(src, dst, out_sem.at[n])
        for n, (src, dst) in enumerate(
            ((v_filter, out_filter), (v_first, out_first), (v_second, out_second))
        )
    ]
    copies[0].start()
    for x, w, dst, copy in ((fg, c1, v_first, copies[1]), (sg, c2, v_second, copies[2])):
        dst[...] = (
            w[0:1, :] * x[0:TOK, :]
            + w[1:2, :] * x[1 : TOK + 1, :]
            + w[2:3, :] * x[2 : TOK + 2, :]
        ).astype(bf16)
        copy.start()
    for chunk in range(CHUNKS):
        all_sent(returned, chunk)
    for copy in copies:
        copy.wait()


def body(pf, ps, og, up, fr, c1, c2, sk):
    hbm = pl.BlockSpec(memory_space=pltpu.HBM)
    dma = pltpu.SemaphoreType.DMA
    return pl.pallas_call(
        kernel,
        out_shape=(
            jax.ShapeDtypeStruct((TOK, LANES), bf16),
            jax.ShapeDtypeStruct((TOK, LANES), bf16),
            jax.ShapeDtypeStruct((TOK, LANES), f32),
        ),
        in_specs=[hbm] * 8,
        out_specs=(hbm,) * 3,
        scratch_shapes=[
            *[pltpu.VMEM((TOK, LANES), bf16)] * 2,
            pltpu.VMEM((TOK, LANES), f32),
            *[pltpu.VMEM((TOK, LANES), bf16)] * 5,
            *[pltpu.VMEM((3, LANES), f32)] * 2,
            pltpu.VMEM((1, LANES), f32),
            pltpu.VMEM((6, EDGE, LANES), bf16),
            pltpu.VMEM((CHUNKS, N, ROWS + 16, LANES), bf16),
            pltpu.VMEM((CHUNKS, N, ROWS + 16, LANES), bf16),
            pltpu.VMEM((CHUNKS - 1, 64 * OWN, LANES), bf16),
            pltpu.VMEM((CHUNKS, N, HOME + 16, LANES), bf16),
            pltpu.VMEM((CHUNKS, 4, LANES, LANES), bf16),
            pltpu.VMEM((512, 512), bf16),
            pltpu.VMEM((N, HOME + 16, LANES), bf16),
            pltpu.VMEM((N, OWN, LANES), f32),
            pltpu.VMEM((N, OWN, LANES), f32),
            pltpu.VMEM((EDGE + EXT, LANES), f32),
            pltpu.VMEM((EDGE + EXT, LANES), f32),
            pltpu.VMEM((EXT, LANES), f32),
            pltpu.VMEM((EXT, LANES), f32),
            pltpu.VMEM((EXT, LANES), bf16),
            pltpu.VMEM((EXT, LANES), f32),
            pltpu.VMEM((EXT, LANES), f32),
            pltpu.VMEM((33, OWN, LANES), f32),
            pltpu.VMEM((2, 32, OWN, LANES), f32),
            pltpu.VMEM((2, 2, 2, 128, LANES), f32),
            pltpu.VMEM((2, 16, 2, 2, 112, LANES), bf16),
            pltpu.VMEM((2, 2, 2, 64, 3 * LANES), f32),
            pltpu.VMEM((72, OWN, LANES), f32),
            dma((6,)),
            dma((6,)),
            dma((2 * CHUNKS, N)),
            dma((2 * CHUNKS, N)),
            dma((2 * CHUNKS,)),
            dma((8,)),
            dma((3,)),
        ],
        compiler_params=pltpu.CompilerParams(
            collective_id=0, has_side_effects=True, vmem_limit_bytes=56 * 2**20
        ),
        cost_estimate=pl.CostEstimate(
            flops=2 * 4 * 10**9, bytes_accessed=3 * 10**6, transcendentals=0
        ),
    )(pf, ps, og, up, fr, c1, c2, sk.reshape(1, LANES))


def solution(mesh):
    tok = P("seq", "ch")
    return jax.shard_map(
        body,
        mesh=mesh,
        in_specs=(tok,) * 5 + (P(None, "ch"), P(None, "ch"), P("ch")),
        out_specs=(tok,) * 3,
        check_vma=False,
    )
```

```python
from functools import partial

import jax
import jax.numpy as jnp
from jax import lax
from jax.experimental import pallas as pl
from jax.experimental.pallas import tpu as pltpu
from jax.sharding import PartitionSpec as P

f32 = jnp.float32
bf16 = jnp.bfloat16
MESH = pl.DeviceIdType.MESH
N = 16
LANES = 128
TOK = 1024
EXT = TOK + 16
OWN = 8
CHUNKS = 4
ROWS = 48
HOME = 32
EDGE = 16


PARTNERS = sorted(
    ((x, z, c) for x in range(2) for z in range(4) for c in range(2) if x + z + c),
    key=lambda k: -2 * k[0] - min(k[1], 4 - k[1]),
)


def partner(me, k):
    x = lax.rem(me // 8 + k[0], 2)
    z = lax.rem(lax.rem(me // 2, 4) + k[1], 4)
    return 8 * x + 2 * z + lax.rem(lax.rem(me, 2) + k[2], 2)


def kernel(
    pf_in, ps_in, og_in, up_in, fr_in, c1_in, c2_in, sk_in,
    out_first, out_second, out_filter,
    v_first, v_second, v_filter,
    pf, ps, og, up, fr, c1, c2, sk,
    halo, sbuf, rbuf, ybuf, rret, tok, pick, ylast, first, heads,
    pfx, psx, fc, sc, gg, fg, sg,
    gin, fin, frps, lss, accs, y,
    halo_send, halo_recv, send_sem, recv_sem, local_sem, in_sem, out_sem,
):
    me = lax.axis_index("seq")
    nxt = lax.rem(me + 1, N)
    prv = lax.rem(me + N - 1, N)

    barrier = pltpu.get_barrier_semaphore()

    def greet(k, _):
        pl.semaphore_signal(
            barrier, inc=1, device_id={"seq": lax.rem(me + k, N)}, device_id_type=MESH
        )
        return 0

    lax.fori_loop(1, N, greet, 0)

    fetched = [
        pltpu.make_async_copy(src, dst, in_sem.at[n])
        for n, (src, dst) in enumerate(
            (
                (og_in, og),
                (up_in, up),
                (fr_in, fr),
                (pf_in, pf),
                (ps_in, ps),
                (c1_in, c1),
                (c2_in, c2),
                (sk_in, sk),
            )
        )
    ]
    for copy in fetched:
        copy.start()

    row2 = lax.broadcasted_iota(jnp.int32, (512, 512), 0)
    col2 = lax.broadcasted_iota(jnp.int32, (512, 512), 1)
    picked = ((row2 & 6) << 6) + (row2 & 120) + ((row2 >> 7) << 1) + (row2 & 1)
    pick[...] = (picked == col2).astype(f32).astype(bf16)
    row1 = lax.broadcasted_iota(jnp.int32, (256, 256), 0)
    col1 = lax.broadcasted_iota(jnp.int32, (256, 256), 1)
    source = ((row1 & 64) << 1) + ((row1 >> 7) << 6) + 63 - (row1 & 63)
    flip = (source == col1).astype(f32).astype(bf16)
    eye = (row1 == col1)[0:LANES, 0:LANES].astype(f32).astype(bf16)

    def put(base, pairs):
        wide = [jnp.concatenate(pairs[n : n + 2], axis=1) for n in (0, 2)]
        turned = lax.dot_general(
            pick[...],
            jnp.concatenate(wide, axis=0),
            (((1,), (1,)), ((), ())),
            preferred_element_type=f32,
        )
        both = jnp.concatenate(
            [
                turned[:, LANES * n : LANES * (n + 1)].reshape(CHUNKS, N, OWN, LANES)
                for n in range(2)
            ],
            axis=2,
        ).astype(bf16)
        for chunk in range(CHUNKS):
            sbuf[chunk, :, base : base + 16, :] = both[chunk]

    def backwards(quarters):
        wide = jnp.concatenate(quarters[::-1], axis=1)
        back = jnp.dot(flip, wide, preferred_element_type=f32).astype(bf16)
        return [
            jnp.concatenate(
                [
                    back[LANES * z : LANES * (z + 1), LANES * q : LANES * (q + 1)]
                    for z in range(2)
                ],
                axis=1,
            )
            for q in range(len(quarters))
        ]

    def paired(blocks):
        return [jnp.concatenate(blocks[n : n + 2], axis=1) for n in range(0, len(blocks), 2)]

    def blocks_of(ref, size):
        return [ref[size * i : size * (i + 1), :] for i in range(TOK // size)]

    partners = [partner(me, k) for k in PARTNERS]

    def sent(chunk, to, frm):
        part = pl.ds(0, ROWS + 16 if isinstance(chunk, int) and chunk == 0 else ROWS)
        return sbuf.at[chunk, to, part], rbuf.at[chunk, frm, part]

    def exchange(chunk):
        for to in partners:
            src, dst = sent(chunk, to, me)
            pltpu.make_async_remote_copy(
                src_ref=src,
                dst_ref=dst,
                send_sem=send_sem.at[chunk, to],
                recv_sem=recv_sem.at[chunk, me],
                device_id={"seq": to},
                device_id_type=MESH,
            ).start()
        src, dst = sent(chunk, me, me)
        pltpu.make_async_copy(src, dst, local_sem.at[chunk]).start()

    def expected(chunk, frm):
        src, dst = sent(chunk, frm, frm)
        return pltpu.make_async_remote_copy(
            src_ref=src,
            dst_ref=dst,
            send_sem=send_sem.at[chunk, frm],
            recv_sem=recv_sem.at[chunk, frm],
            device_id={"seq": frm},
            device_id_type=MESH,
        )

    def all_sent(copy, chunk):
        def go(k, _):
            copy(chunk, lax.rem(me + k, N)).wait_send()
            return 0

        lax.fori_loop(1, N, go, 0)

    def arrived(chunk):
        def go(k, _):
            expected(chunk, lax.rem(me + k, N)).wait_recv()
            return 0

        src, dst = sent(chunk, me, me)
        pltpu.make_async_copy(src, dst, local_sem.at[chunk]).wait()
        lax.fori_loop(1, N, go, 0)

    fetched[0].wait()
    fetched[1].wait()
    gg[0:TOK, :] = (og[...].astype(f32) * up[...].astype(f32)).astype(bf16)
    put(0, paired(blocks_of(gg, LANES)))
    fetched[2].wait()
    put(16, backwards(blocks_of(fr, 256)))

    for copy in fetched[3:]:
        copy.wait()

    def convolve(start, size):
        for x, w, dst in ((pfx, c1, fc), (psx, c2, sc)):
            dst[start : start + size, :] = (
                w[0:1, :] * x[EDGE + start : EDGE + start + size, :]
                + w[1:2, :] * x[EDGE + start - 1 : EDGE + start - 1 + size, :]
                + w[2:3, :] * x[EDGE + start - 2 : EDGE + start - 2 + size, :]
            )

    def products(quarters):
        return [
            (fc[256 * q : 256 * (q + 1), :] * sc[256 * q : 256 * (q + 1), :]).astype(bf16)
            for q in quarters
        ]

    for x, src in ((pfx, pf), (psx, ps)):
        x[EDGE : EDGE + TOK, :] = src[...].astype(f32)
    for x in (pfx, psx):
        x[0:EDGE, :] = jnp.zeros((EDGE, LANES), f32)
    convolve(0, TOK)
    put(32, backwards(products(range(4))))
    row3 = lax.broadcasted_iota(jnp.int32, (LANES, 2 * EDGE), 0)
    col3 = lax.broadcasted_iota(jnp.int32, (LANES, 2 * EDGE), 1)
    head = (row3 + col3 == 63) & (col3 < 2)
    tail = (row3 - col3 == 127 - 31) & (col3 >= 30)
    edge_pick = (head | tail).astype(f32).astype(bf16)
    edges = jnp.concatenate(
        [
            jnp.dot(
                edge_pick,
                jnp.concatenate([x[0:EDGE, :], x[TOK - EDGE : TOK, :]], axis=0),
                preferred_element_type=f32,
            ).astype(bf16)
            for x in (pf, ps)
        ],
        axis=0,
    )
    turned = [
        lax.dot_general(
            eye,
            edges[LANES * z : LANES * (z + 1)],
            (((1,), (1,)), ((), ())),
            preferred_element_type=f32,
        ).reshape(N, OWN, LANES)
        for z in range(2)
    ]
    sbuf[0, :, ROWS : ROWS + 16, :] = jnp.concatenate(turned, axis=1).astype(bf16)

    pl.semaphore_wait(barrier, N - 1)

    halos = [
        (pf_in, TOK - EDGE, nxt),
        (ps_in, TOK - EDGE, nxt),
        (pf_in, 0, prv),
        (ps_in, 0, prv),
        (og_in, 0, prv),
        (up_in, 0, prv),
    ]
    halo_copies = [
        pltpu.make_async_remote_copy(
            src_ref=ref.at[pl.ds(start, EDGE), :],
            dst_ref=halo.at[n],
            send_sem=halo_send.at[n],
            recv_sem=halo_recv.at[n],
            device_id={"seq": to},
            device_id_type=MESH,
        )
        for n, (ref, start, to) in enumerate(halos)
    ]

    for chunk in range(CHUNKS):
        exchange(chunk)
    for copy in halo_copies:
        copy.start()

    frps[...] = jnp.zeros_like(frps)
    gin[32] = jnp.zeros((OWN, LANES), f32)
    y[64] = jnp.zeros((OWN, LANES), f32)

    def unpack_gated(chunk):
        rows = rbuf[chunk, :, 0:16, :].astype(f32)
        gin[0:32, :, :] = rows.reshape(32, OWN, LANES)

    lane = lax.broadcasted_iota(jnp.int32, (OWN, LANES), 1)
    place = lax.broadcasted_iota(jnp.int32, (OWN, LANES), 0)

    def taps(ref):
        mine = lane == OWN * me + place
        for k in range(3):
            yield jnp.sum(jnp.where(mine, ref[k : k + 1, :], 0.0), axis=1, keepdims=True)

    def unpack_edges():
        weights = [list(taps(ref)) for ref in (c1, c2)]
        at63 = lane == 63
        last = [jnp.zeros((OWN, LANES), f32)] * 2
        for s in range(N):
            rows = rbuf[0, s, ROWS : ROWS + 16, :].astype(f32)
            conv = []
            for z in range(2):
                own = rows[OWN * z : OWN * (z + 1)]
                w = weights[z]
                one = jnp.where(at63, last[z], pltpu.roll(own, LANES - 1, 1))
                two = jnp.where(
                    at63, pltpu.roll(last[z], 1, 1), pltpu.roll(last[z], LANES - 1, 1)
                )
                conv.append(w[0] * own + w[1] * one + w[2] * two)
                last[z] = pltpu.roll(own, 64, 1)
            first[N - 1 - s] = (conv[0] * conv[1]).astype(bf16).astype(f32)

    def unpack_filter(chunk, f):
        for s in range(N):
            rows = rbuf[chunk, N - 1 - s, 16 * f + 16 : 16 * f + 32, :].astype(f32)
            fin[f, 2 * s : 2 * s + 2, :, :] = rows.reshape(2, OWN, LANES)

    row = lax.broadcasted_iota(jnp.int32, (64, LANES), 0)
    col = lax.broadcasted_iota(jnp.int32, (64, LANES), 1)
    mask = col - row <= 64
    low = col < 64
    fill = ((col == 62) | (col == 63))[0:N]

    def rolled(jj, ch):
        line = gin[jj // 4, pl.ds(2 * (jj % 4) + ch, 1), :]
        return pltpu.roll(
            jnp.broadcast_to(line, (64, LANES)), 65, 1, stride=1, stride_axis=0
        )

    def channel(ch, chunk):
        frp, ls, acc = frps.at[ch], lss.at[ch], accs.at[ch]
        for z in range(2):
            for f in range(2):
                for u in range(2):
                    frp[z, f, pl.ds(u, 32, stride=2), :] = fin[f, :, 4 * u + 2 * z + ch, :]
        at = pl.ds(3, N, stride=4)
        frp[0, 1, at, :] = jnp.where(
            fill, first[:, 2 * chunk + ch, :], frp[0, 1, at, :]
        )
        for r in range(16):
            for z in range(2):
                for f in range(2):
                    ls[r, z, f] = frp[z, f, pl.ds(r, 112), :].astype(bf16)
        acc[...] = jnp.zeros_like(acc)
        lines = [rolled(0, ch)]
        hankel = []

        def more_blocks(count):
            while len(hankel) < count:
                lines.append(rolled(min(len(lines), 128), ch))
                hankel.append(jnp.where(mask, lines[-2], lines[-1]).astype(bf16))

        for group in range(4):
            rows = 16 * (group + 1)
            top = 16 * (3 - group)
            left, right = [], []
            for k in range(16):
                j = 16 * group + k
                left.append(ls[15 - k, :, :, top : top + rows, :].reshape(4 * rows, LANES))
                more_blocks(2 * j + 4)
                for n in (2 * j, 2 * j + 1):
                    right.append(jnp.concatenate(hankel[n : n + 3], axis=1))
            left = jnp.concatenate(left, axis=1)
            right = jnp.concatenate(right, axis=0)
            both = jnp.dot(left, right[:, 0:256], preferred_element_type=f32)
            more = jnp.dot(left[2 * rows :], right[:, 256:], preferred_element_type=f32)
            acc[:, :, 0:rows, 0:256] += both.reshape(2, 2, rows, 256)
            acc[1, :, 0:rows, 256:] += more.reshape(2, rows, LANES)
        for f in range(2):
            moved = [
                pltpu.roll(acc[1, f, :, LANES * n : LANES * (n + 1)], 64, 1)
                for n in range(3)
            ]
            for h in range(2):
                total = acc[0, f, :, LANES * h : LANES * (h + 1)] + jnp.where(
                    low, moved[h], moved[h + 1]
                )
                y[0:64, 4 * h + 2 * f + ch, :] = total * (1.0, (TOK * N) ** -0.5)[f]
        heads[:, 2 * chunk + ch, :] = y[pl.ds(4, N, stride=4), ch, :]

    def home(chunk, to, frm):
        if isinstance(chunk, int) and chunk == CHUNKS - 1:
            return ylast.at[to], rret.at[chunk, frm]
        rows = pl.ds(pl.multiple_of(HOME * to, HOME), HOME)
        return ybuf.at[chunk, rows, :], rret.at[chunk, frm, pl.ds(0, HOME)]

    def back(chunk):
        for to in partners:
            src, dst = home(chunk, to, me)
            pltpu.make_async_remote_copy(
                src_ref=src,
                dst_ref=dst,
                send_sem=send_sem.at[CHUNKS + chunk, to],
                recv_sem=recv_sem.at[CHUNKS + chunk, me],
                device_id={"seq": to},
                device_id_type=MESH,
            ).start()
        src, dst = home(chunk, me, me)
        pltpu.make_async_copy(src, dst, local_sem.at[CHUNKS + chunk]).start()

    def returned(chunk, frm):
        src, dst = home(chunk, frm, frm)
        return pltpu.make_async_remote_copy(
            src_ref=src,
            dst_ref=dst,
            send_sem=send_sem.at[CHUNKS + chunk, frm],
            recv_sem=recv_sem.at[CHUNKS + chunk, frm],
            device_id={"seq": frm},
            device_id_type=MESH,
        )

    def back_done(chunk):
        def go(k, _):
            returned(chunk, lax.rem(me + k, N)).wait_recv()
            return 0

        src, dst = home(chunk, me, me)
        pltpu.make_async_copy(src, dst, local_sem.at[CHUNKS + chunk]).wait()
        lax.fori_loop(1, N, go, 0)

    def one_chunk(chunk, _):
        @pl.when(chunk > 0)
        def _():
            arrived(chunk)

        unpack_gated(chunk)
        unpack_filter(chunk, 0)
        unpack_filter(chunk, 1)
        for ch in range(2):
            channel(ch, chunk)

        @pl.when(chunk < CHUNKS - 1)
        def _():
            ybuf[chunk] = y[0:64].reshape(64 * OWN, LANES).astype(bf16)
            back(chunk)

        return 0

    arrived(0)
    unpack_edges()
    lax.fori_loop(0, CHUNKS, one_chunk, 0)
    ylast[:, 0:HOME, :] = y[0:64].reshape(N, HOME, LANES).astype(bf16)
    ylast[:, HOME:, :] = jnp.concatenate([heads[...]] * 2, axis=1).astype(bf16)
    back(CHUNKS - 1)
    for chunk in range(CHUNKS):
        all_sent(expected, chunk)

    for copy in halo_copies:
        copy.wait()
    before = me > 0
    after = me < N - 1
    for n, x in enumerate((pfx, psx)):
        x[0:EDGE, :] = jnp.where(before, halo[n].astype(f32), 0.0)
        x[EDGE + TOK :, :] = halo[n + 2].astype(f32)
    convolve(0, EDGE)
    convolve(TOK, EXT - TOK)
    gg[TOK:, :] = jnp.where(after, halo[4].astype(f32) * halo[5].astype(f32), 0.0).astype(bf16)

    def columns(chunk, pair):
        both = rret[chunk, :, 16 * pair : 16 * pair + 16, :].astype(f32)
        both = both.reshape(N, 2, OWN, LANES)
        for n in range(2):
            turned = jnp.transpose(both[:, n].reshape(LANES, LANES))
            tok[chunk, 2 * pair + n] = turned.astype(bf16)

    skip = sk[...]

    def grads(start, size, mix):
        at = pl.ds(start, size)
        total = mix + skip * gg[at, :].astype(f32)
        fg[at, :] = (total * sc[at, :]).astype(bf16).astype(f32)
        sg[at, :] = (total * fc[at, :]).astype(bf16).astype(f32)

    for chunk in range(CHUNKS):
        back_done(chunk)
        for pair in range(2):
            columns(chunk, pair)
    following = rret[CHUNKS - 1, :, HOME:, :].astype(f32)[:, 0:OWN].reshape(LANES, LANES)
    grads(TOK, EXT - TOK, jnp.transpose(following)[0 : EXT - TOK])
    for i in range(4):
        both = jnp.dot(
            jnp.concatenate([tok[chunk, i] for chunk in range(CHUNKS)], axis=1),
            pick[...],
            preferred_element_type=f32,
        )
        for h in range(2):
            at = 256 * i + LANES * h
            grads(at, LANES, both[:, 256 * h : 256 * h + LANES])
            v_filter[at : at + LANES, :] = both[:, 256 * h + LANES : 256 * h + 256]
    copies = [
        pltpu.make_async_copy(src, dst, out_sem.at[n])
        for n, (src, dst) in enumerate(
            ((v_filter, out_filter), (v_first, out_first), (v_second, out_second))
        )
    ]
    copies[0].start()
    for x, w, dst, copy in ((fg, c1, v_first, copies[1]), (sg, c2, v_second, copies[2])):
        dst[...] = (
            w[0:1, :] * x[0:TOK, :]
            + w[1:2, :] * x[1 : TOK + 1, :]
            + w[2:3, :] * x[2 : TOK + 2, :]
        ).astype(bf16)
        copy.start()
    for chunk in range(CHUNKS):
        all_sent(returned, chunk)
    for copy in copies:
        copy.wait()


def body(pf, ps, og, up, fr, c1, c2, sk):
    hbm = pl.BlockSpec(memory_space=pltpu.HBM)
    dma = pltpu.SemaphoreType.DMA
    return pl.pallas_call(
        kernel,
        out_shape=(
            jax.ShapeDtypeStruct((TOK, LANES), bf16),
            jax.ShapeDtypeStruct((TOK, LANES), bf16),
            jax.ShapeDtypeStruct((TOK, LANES), f32),
        ),
        in_specs=[hbm] * 8,
        out_specs=(hbm,) * 3,
        scratch_shapes=[
            *[pltpu.VMEM((TOK, LANES), bf16)] * 2,
            pltpu.VMEM((TOK, LANES), f32),
            *[pltpu.VMEM((TOK, LANES), bf16)] * 5,
            *[pltpu.VMEM((3, LANES), f32)] * 2,
            pltpu.VMEM((1, LANES), f32),
            pltpu.VMEM((6, EDGE, LANES), bf16),
            pltpu.VMEM((CHUNKS, N, ROWS + 16, LANES), bf16),
            pltpu.VMEM((CHUNKS, N, ROWS + 16, LANES), bf16),
            pltpu.VMEM((CHUNKS - 1, 64 * OWN, LANES), bf16),
            pltpu.VMEM((CHUNKS, N, HOME + 16, LANES), bf16),
            pltpu.VMEM((CHUNKS, 4, LANES, LANES), bf16),
            pltpu.VMEM((512, 512), bf16),
            pltpu.VMEM((N, HOME + 16, LANES), bf16),
            pltpu.VMEM((N, OWN, LANES), f32),
            pltpu.VMEM((N, OWN, LANES), f32),
            pltpu.VMEM((EDGE + EXT, LANES), f32),
            pltpu.VMEM((EDGE + EXT, LANES), f32),
            pltpu.VMEM((EXT, LANES), f32),
            pltpu.VMEM((EXT, LANES), f32),
            pltpu.VMEM((EXT, LANES), bf16),
            pltpu.VMEM((EXT, LANES), f32),
            pltpu.VMEM((EXT, LANES), f32),
            pltpu.VMEM((33, OWN, LANES), f32),
            pltpu.VMEM((2, 32, OWN, LANES), f32),
            pltpu.VMEM((2, 2, 2, 128, LANES), f32),
            pltpu.VMEM((2, 16, 2, 2, 112, LANES), bf16),
            pltpu.VMEM((2, 2, 2, 64, 3 * LANES), f32),
            pltpu.VMEM((72, OWN, LANES), f32),
            dma((6,)),
            dma((6,)),
            dma((2 * CHUNKS, N)),
            dma((2 * CHUNKS, N)),
            dma((2 * CHUNKS,)),
            dma((8,)),
            dma((3,)),
        ],
        compiler_params=pltpu.CompilerParams(
            collective_id=0, has_side_effects=True, vmem_limit_bytes=56 * 2**20
        ),
        cost_estimate=pl.CostEstimate(
            flops=2 * 4 * 10**9, bytes_accessed=3 * 10**6, transcendentals=0
        ),
    )(pf, ps, og, up, fr, c1, c2, sk.reshape(1, LANES))


def solution(mesh):
    tok = P("seq", "ch")
    return jax.shard_map(
        body,
        mesh=mesh,
        in_specs=(tok,) * 5 + (P(None, "ch"), P(None, "ch"), P("ch")),
        out_specs=(tok,) * 3,
        check_vma=False,
    )
```
